512 devices in a mesh: gx: 8 (over y, z_hi), gy: 16 (over z_lo, core), frame: 4 (over x).
Axes of the slice: x: 4, y: 4, z: 16 (z_hi: 2, z_lo: 8; z = z_hi * 8 + z_lo), core: 2. Of those that a mesh axis runs over, the one named last changes fastest.
Arguments:
- features: bfloat16 [32, 32, 128, 128], P(('frame', 'gx'), 'gy'), parts along dimension 0, may hold values from -6 to 6
- positions: float32 [32, 32, 3, 128], P(('frame', 'gx'), 'gy'), parts along dimension 0, may hold values from 0 to 1
- bead_types: int32 [32, 32, 128], P(('frame', 'gx'), 'gy'), parts along dimension 0, may hold values from 0 to 15
- cell_counts: int32 [32, 32], P(('frame', 'gx'), 'gy'), parts along dimension 0, may hold values from 48 to 128
- w_value: bfloat16 [128, 128], replicated, may hold values from -0.5 to 0.5
- w_radial: float32 [8, 128], replicated, may hold values from -0.6 to 0.6
- type_gain: float32 [16, 128], replicated, may hold values from 0.1 to 1.9
- w_out: bfloat16 [128, 128], replicated, may hold values from -0.5 to 0.5
- cotangent: bfloat16 [32, 32, 128, 128], P(('frame', 'gx'), 'gy'), parts along dimension 0, may hold values from -6 to 6
Outputs:
- out_feat: bfloat16 [32, 32, 128, 128], P(('frame', 'gx'), 'gy'), parts along dimension 0
- grad_feat: bfloat16 [32, 32, 128, 128], P(('frame', 'gx'), 'gy'), parts along dimension 0
- grad_pos: float32 [32, 32, 3, 128], P(('frame', 'gx'), 'gy'), parts along dimension 0
- grad_wvalue: float32 [512, 128], P('frame'), parts along dimension 0
- grad_wradial: float32 [32, 128], P('frame'), parts along dimension 0
- grad_gain: float32 [64, 128], P('frame'), parts along dimension 0
- grad_wout: float32 [512, 128], P('frame'), parts along dimension 0
The draws below stay inside these ranges and needn't reach their ends.
There are 4 independent parts, one for each index of `frame`. The reference program is written for one: setup_inputs(seed, part) draws one part's arguments, and reference() takes and returns one part's arrays. A program takes and returns all parts, laid end to end along the dimension named above; an argument that names none is the same for every part. Nothing has to cross between parts.
All inputs are finite; a program needn't handle non-finite values.
Results may differ from the reference program's by a relative error of at most 0.012.
Values may be sent and summed in bfloat16 or wider, within the bound.
A program may use at most 64 MiB of HBM per device.

```python
import jax
import jax.numpy as jnp
from jax import lax

C = 128
B = 8
P_SIZE = 128
NT = 16
HZ = 6
NCX = 8
NCY = 32


def place_ends(result, rng, smallest, top_value):
    index_at = [jax.random.randint(jax.random.fold_in(rng, axis), (), 0, length) for axis, length in enumerate(result.shape)]
    main_axis = result.shape.index(max(result.shape))
    beside = index_at[:main_axis] + [(index_at[main_axis] + 1) % result.shape[main_axis]] + index_at[main_axis + 1:]
    return result.at[tuple(index_at)].set(smallest).at[tuple(beside)].set(top_value)


def block_scale(own_key, extent, shards, low, high):
    level = 1.0
    for position, blocks in shards:
        draws = jax.random.uniform(jax.random.fold_in(jax.random.fold_in(own_key, 6), position), (blocks,), jnp.float32, low / len(shards), high / len(shards))
        level = level * jnp.repeat(jnp.exp(draws), extent[position] // blocks).reshape((-1,) + (1,) * (len(extent) - 1 - position))
    return level


def scatter_about(rng, extent, deviation, limit, pieces=(), held_as=jnp.bfloat16):
    gain = block_scale(rng, extent, pieces, -0.22, 0.18) if pieces else 1.0
    drawn = jax.random.normal(rng, extent, jnp.float32) * deviation * gain
    return jnp.minimum(jnp.maximum(drawn, -limit), limit).astype(held_as)


def setup_inputs(seed: int = 0, part: int = 0) -> dict:
    key_list = jax.random.split(jax.random.key(seed), 10)
    part_keys = jax.random.split(jax.random.fold_in(key_list[9], part), 10)
    features = scatter_about(part_keys[0], (NCX, NCY, P_SIZE, C), 1.0, 6.0, ((0, 8), (1, 16)))
    positions = jnp.clip(1.0 * jax.random.uniform(part_keys[1], (NCX, NCY, 3, P_SIZE), jnp.float32) ** block_scale(part_keys[1], (NCX, NCY, 3, P_SIZE), ((0, 8), (1, 16)), -0.2, 0.2), 0.0, 1.0)
    bead_types = place_ends(jax.random.randint(part_keys[2], (NCX, NCY, P_SIZE), 0, NT), jax.random.fold_in(part_keys[2], 1), 0, NT - 1).astype(jnp.int32)
    cell_counts = place_ends(jax.random.randint(part_keys[3], (NCX, NCY), P_SIZE * 3 // 8, P_SIZE + 1), jax.random.fold_in(part_keys[3], 1), P_SIZE * 3 // 8, P_SIZE).astype(jnp.int32)
    w_value = scatter_about(key_list[4], (C, C), C ** -0.5, 0.5)
    w_radial = scatter_about(key_list[5], (B, C), 0.1, 0.6, (), jnp.float32)
    type_gain = jnp.clip(1.0 + 0.18 * jax.random.normal(key_list[6], (NT, C), jnp.float32), 0.1, 1.9)
    w_out = scatter_about(key_list[7], (C, C), C ** -0.5, 0.5)
    cotangent = scatter_about(part_keys[8], (NCX, NCY, P_SIZE, C), 1.0, 6.0, ((0, 8), (1, 16)))
    return {"features": features, "positions": positions, "bead_types": bead_types, "cell_counts": cell_counts, "w_value": w_value, "w_radial": w_radial, "type_gain": type_gain, "w_out": w_out, "cotangent": cotangent}


soften = 0.01
stencil = [(-1, -1), (-1, 0), (-1, 1), (0, -1), (0, 0), (0, 1), (1, -1), (1, 0), (1, 1)]

def pair_terms(pos_own, pos_near, shift_x, shift_y, is_self, basis_count):
    slot_count = pos_own.shape[-1]
    offsets = (float(shift_x), float(shift_y), 0.0)
    scales = (1.0, 1.0, float(HZ))
    deltas = [(pos_near[:, :, component, None, :] - pos_own[:, :, component, :, None]) * scales[component] + offsets[component] for component in range(3)]
    dist_sq = deltas[0] * deltas[0] + deltas[1] * deltas[1] + deltas[2] * deltas[2]
    pair_mask = pos_own[:, :, 3, :, None] * pos_near[:, :, 3, None, :]
    if is_self:
        pair_mask = pair_mask * (1.0 - jnp.eye(slot_count, dtype=jnp.float32))
    radius = jnp.sqrt(dist_sq + soften)
    inside = jnp.maximum(1.0 - dist_sq, 0.0)
    envelope = inside * inside
    centres = jnp.arange(basis_count, dtype=jnp.float32) / (basis_count - 1)
    width_gamma = 0.5 * (basis_count - 1) ** 2
    offset_r = radius[:, :, None] - centres[None, None, :, None, None]
    gaussian = jnp.exp(-width_gamma * offset_r * offset_r)
    weights = ((pair_mask * envelope)[:, :, None] * gaussian).astype(jnp.bfloat16)
    slope_r2 = pair_mask[:, :, None] * gaussian * (-2.0 * inside[:, :, None] - envelope[:, :, None] * width_gamma * offset_r / radius[:, :, None])
    scaled_deltas = [deltas[component] * scales[component] for component in range(3)]
    return (weights, slope_r2, scaled_deltas)

def reference(features, positions, bead_types, cell_counts, w_value, w_radial, type_gain, w_out, cotangent):
    cells_x, cells_y, slot_count, channels = features.shape
    basis_count = w_radial.shape[0]
    valid_slot = (jnp.arange(slot_count, dtype=jnp.int32)[None, None, :] < cell_counts[:, :, None]).astype(jnp.float32)
    pos_valid = jnp.concatenate([positions, valid_slot[:, :, None, :]], axis=2)
    flat_feat = features.reshape(-1, channels)
    projected = jnp.dot(flat_feat, w_value, preferred_element_type=jnp.float32)
    onehot = (bead_types.reshape(-1)[:, None] == jnp.arange(type_gain.shape[0], dtype=jnp.int32)[None, :]).astype(jnp.float32)
    bead_gain = jnp.dot(onehot, type_gain, precision=lax.Precision.HIGHEST)
    carried = (projected * bead_gain).astype(jnp.bfloat16).reshape(cells_x, cells_y, slot_count, channels)
    summed = jnp.zeros((cells_x, cells_y, basis_count, slot_count, channels), jnp.float32)
    for shift_x, shift_y in stencil:
        near_pos = jnp.roll(pos_valid, (-shift_x, -shift_y), axis=(0, 1))
        near_val = jnp.roll(carried, (-shift_x, -shift_y), axis=(0, 1))
        weights, slope_r2, deltas = pair_terms(pos_valid, near_pos, shift_x, shift_y, shift_x == 0 and shift_y == 0, basis_count)
        summed = summed + jnp.einsum('abkij,abjc->abkic', weights.astype(jnp.float32), near_val.astype(jnp.float32))
    aggregate = lax.optimization_barrier(jnp.sum(summed * w_radial[None, None, :, None, :], axis=2))
    agg_half = aggregate.astype(jnp.bfloat16).reshape(-1, channels)
    pre_act = jnp.dot(agg_half, w_out, preferred_element_type=jnp.float32)
    sigmoid_act = jax.nn.sigmoid(pre_act)
    out_feat = (flat_feat.astype(jnp.float32) + pre_act * sigmoid_act).astype(jnp.bfloat16)
    grad_pre = (cotangent.reshape(-1, channels).astype(jnp.float32) * sigmoid_act * (1.0 + pre_act * (1.0 - sigmoid_act))).astype(jnp.bfloat16)
    grad_wout = jnp.dot(agg_half.T, grad_pre, preferred_element_type=jnp.float32)
    grad_agg = jnp.dot(grad_pre, w_out.T, preferred_element_type=jnp.float32).astype(jnp.bfloat16).reshape(cells_x, cells_y, slot_count, channels)
    grad_wradial = lax.optimization_barrier(jnp.sum(summed * grad_agg.astype(jnp.float32)[:, :, None], axis=(0, 1, 3)))
    scaled = (grad_agg.astype(jnp.float32)[:, :, None] * w_radial[None, None, :, None, :]).astype(jnp.bfloat16)
    grad_carried = jnp.zeros((cells_x, cells_y, slot_count, channels), jnp.float32)
    grad_pos = jnp.zeros((cells_x, cells_y, 3, slot_count), jnp.float32)
    for shift_x, shift_y in stencil:
        near_pos = jnp.roll(pos_valid, (-shift_x, -shift_y), axis=(0, 1))
        near_val = jnp.roll(carried, (-shift_x, -shift_y), axis=(0, 1))
        weights, slope_r2, deltas = pair_terms(pos_valid, near_pos, shift_x, shift_y, shift_x == 0 and shift_y == 0, basis_count)
        weight_grad = jnp.einsum('abkic,abjc->abkij', scaled.astype(jnp.float32), near_val.astype(jnp.float32))
        pair_pull = lax.optimization_barrier(jnp.sum(weight_grad * slope_r2, axis=2))
        own_pull = jnp.stack([-2.0 * lax.optimization_barrier(jnp.sum(pair_pull * delta_one, axis=3)) for delta_one in deltas], axis=2)
        far_pull = jnp.stack([2.0 * lax.optimization_barrier(jnp.sum(pair_pull * delta_one, axis=2)) for delta_one in deltas], axis=2)
        far_value = jnp.einsum('abkij,abkic->abjc', weights.astype(jnp.float32), scaled.astype(jnp.float32))
        grad_pos = grad_pos + own_pull + jnp.roll(far_pull, (shift_x, shift_y), axis=(0, 1))
        grad_carried = grad_carried + jnp.roll(far_value, (shift_x, shift_y), axis=(0, 1))
    flat_carried = grad_carried.reshape(-1, channels)
    grad_half = (flat_carried * bead_gain).astype(jnp.bfloat16)
    grad_feat = (cotangent.reshape(-1, channels).astype(jnp.float32) + jnp.dot(grad_half, w_value.T, preferred_element_type=jnp.float32)).astype(jnp.bfloat16)
    grad_wvalue = jnp.dot(flat_feat.T, grad_half, preferred_element_type=jnp.float32)
    grad_gain = jnp.dot(onehot.T, flat_carried * projected, precision=lax.Precision.HIGHEST)
    return (out_feat.reshape(cells_x, cells_y, slot_count, channels), grad_feat.reshape(cells_x, cells_y, slot_count, channels), grad_pos, grad_wvalue, grad_wradial, grad_gain, grad_wout)
```

```python
import jax
import jax.numpy as jnp
from jax import lax
from jax.experimental import pallas as pl
from jax.experimental.pallas import tpu as pltpu
from jax.sharding import PartitionSpec as P

MESH = pl.DeviceIdType.MESH
F32 = jnp.float32
BF16 = jnp.bfloat16
HZ = 6.0
SOFTEN = 0.01
N = 128
K = 8
NX = 8
NY = 16
GAMMA = 24.5
FAR = 1000.0
POS, VAL, GRAD = 0, 1, 2
ROWS = 16

FIRST = (
    ((0, 1), (1, 1), "O"),
    ((0, 2), (1, 2), "O"),
    ((0, 1), (0, 3), "W"),
    ((0, 2), (0, 0), "E"),
)
RELAY = {
    1: (((1, 1), (2, 1), "P"), ((1, 1), (1, 3), "W"), ((1, 1), (2, 3), "PW")),
    2: (((1, 2), (2, 2), "P"), ((1, 2), (1, 0), "E"), ((1, 2), (2, 0), "PE")),
}


def dot(a, b, dims=((1,), (0,)), precision=None):
    return lax.dot_general(a, b, (dims, ((), ())), precision=precision, preferred_element_type=F32)


def kernel(
    feat, pos, types, counts, w_value, w_radial, type_gain, w_out, cot,
    out_feat, grad_feat, grad_pos, grad_wvalue, grad_wradial, grad_gain, grad_wout,
    hp, hc, hg, own, ebuf, usum, sbuf, lhs, pacc, proj, gain, onehot,
    ar_src, ar_one, ar_mid, ar_two, ar_three,
    send_sem, recv_sem, ar_send, ar_recv,
):
    gx = lax.axis_index("gx")
    gy = lax.axis_index("gy")
    zh = lax.rem(gx, 2)
    yy = gx // 2
    side = 1 - 2 * zh
    side_f = side.astype(F32)
    west, east = lax.rem(gy + NY - 1, NY), lax.rem(gy + 1, NY)
    across = lax.rem(gx + side + NX, NX)
    beyond = lax.rem(gx + 2 * side + NX, NX)
    behind = lax.rem(gx - 2 * side + NX, NX)
    dev = {
        "O": (across, gy), "W": (gx, west), "E": (gx, east), "P": (beyond, gy),
        "PW": (beyond, west), "PE": (beyond, east),
        "Q": (behind, gy), "QW": (behind, west), "QE": (behind, east),
    }
    dev = {name: {"gx": x, "gy": y} for name, (x, y) in dev.items()}
    quad = gy // 4
    q_me = yy * 4 + lax.rem(gy, 4)
    p_me = zh * 4 + quad

    def group_one(q):
        return {"gx": 2 * (q // 4) + zh, "gy": quad * 4 + lax.rem(q, 4)}

    def group_two(p):
        return {"gx": 2 * yy + p // 4, "gy": lax.rem(p, 4) * 4 + lax.rem(gy, 4)}

    barrier = pltpu.get_barrier_semaphore()
    for name in dev:
        pl.semaphore_signal(barrier, inc=1, device_id=dev[name], device_id_type=MESH)

    @pl.loop(1, 16)
    def _(d):
        pl.semaphore_signal(barrier, inc=1, device_id=group_one(lax.rem(q_me + d, 16)), device_id_type=MESH)

    @pl.loop(1, 8)
    def _(d):
        pl.semaphore_signal(barrier, inc=1, device_id=group_two(lax.rem(p_me + d, 8)), device_id_type=MESH)

    lane = lax.broadcasted_iota(jnp.int32, (1, N), 1)
    for c in range(2):
        missing = jnp.where(lane < counts[0, c], 0.0, FAR)
        x, y, z = (pos[0, c, n : n + 1, :] for n in range(3))
        z = z * HZ
        hp[0, :, (1 + c) * N : (2 + c) * N] = jnp.concatenate([x, y, z + missing, jnp.zeros((5, N), F32)], axis=0)
        for n, row in enumerate((x, y, z - missing)):
            own[c, n] = jnp.broadcast_to(row, (N, N)).T
    kind_of = lax.broadcasted_iota(jnp.int32, (16, N), 0)
    for c in range(2):
        hot = jnp.where(kind_of == types[0, c : c + 1, :], 1.0, 0.0)
        onehot[c] = hot
        gain[c] = dot(hot, type_gain[...], ((0,), (0,)), lax.Precision.HIGHEST)
        proj[c] = dot(feat[0, c], w_value[...])
        hc[0, (1 + c) * N : (2 + c) * N, :] = (proj[c] * gain[c]).astype(BF16)

    def slot(kind, place):
        role, column = place
        if kind == POS:
            return hp.at[role, :, column * N : (column + 1) * N]
        return (hc if kind == VAL else hg).at[role, column * N : (column + 1) * N, :]

    sent = []

    def send(kind, messages):
        for src, dst, to in messages:
            copy = pltpu.make_async_remote_copy(
                src_ref=slot(kind, src),
                dst_ref=slot(kind, dst),
                send_sem=send_sem.at[len(sent)],
                recv_sem=recv_sem.at[kind, dst[0] * 4 + dst[1]],
                device_id=dev[to],
                device_id_type=MESH,
            )
            copy.start()
            sent.append(copy)

    def arrive(kind, *places):
        for place in places:
            pltpu.make_async_remote_copy(
                src_ref=slot(kind, place),
                dst_ref=slot(kind, place),
                send_sem=send_sem.at[0],
                recv_sem=recv_sem.at[kind, place[0] * 4 + place[1]],
                device_id=dev["O"],
                device_id_type=MESH,
            ).wait_recv()

    pl.semaphore_wait(barrier, len(dev) + 15 + 7)
    send(POS, FIRST)
    send(VAL, FIRST)

    window = lax.broadcasted_iota(jnp.int32, (1, 3 * N), 1)
    shift_y = (window // N - 1).astype(F32)

    def near(c, role):
        block = hp[role, :, c * N : (c + 3) * N]
        shift_x = (0.0, side_f, -side_f)[role]
        return block[0:1] + shift_x, block[1:2] + shift_y, block[2:3]

    def geometry(c, role, near_rows, i0):
        deltas = []
        for n in range(3):
            mine = own[c, n, pl.ds(i0, ROWS), :]
            deltas.append(near_rows[n] - jnp.concatenate([mine] * 3, axis=1))
        dx, dy, dz = deltas
        dist = dx * dx + dy * dy + dz * dz
        if role == 0:
            row = lax.broadcasted_iota(jnp.int32, (ROWS, 3 * N), 0) + (i0 + N)
            col = lax.broadcasted_iota(jnp.int32, (ROWS, 3 * N), 1)
            dist = jnp.where(row == col, 2.0, dist)
        inside = jnp.maximum(1.0 - dist, 0.0)
        soft = (1.0 + SOFTEN) - inside
        inverse = lax.rsqrt(soft)
        ratio = jnp.exp((K - 1.0) * (soft * inverse))
        base = jnp.exp(-GAMMA * soft)
        return deltas, inside, inverse, ratio, base

    def weights(c, role):
        near_rows = near(c, role)

        @pl.loop(0, N // ROWS)
        def _(i):
            i0 = pl.multiple_of(i * ROWS, ROWS)
            _, inside, _, ratio, base = geometry(c, role, near_rows, i0)
            value = inside * inside * base
            for k in range(K):
                ebuf[c, role, k, pl.ds(i0, ROWS), :] = value.astype(BF16)
                if k < K - 1:
                    value = value * ratio

    def gather(c, role, table, first):
        got = dot(ebuf[c, role].reshape(K * N, 3 * N), table[role, c * N : (c + 3) * N, :]).reshape(K, N, N)
        if first:
            usum[c] = got
        else:
            usum[c] += got

    basis = lax.broadcasted_iota(jnp.int32, (K, N), 0).astype(F32)
    fold = jnp.exp(-0.5 * basis * basis)
    wk = w_radial[...] * fold

    arrive(POS, (0, 0), (0, 3))
    for c in range(2):
        weights(c, 0)
    for col in (1, 2):
        arrive(POS, (1, col))
        send(POS, RELAY[col])
    for c in range(2):
        value = hc[0, (1 + c) * N : (2 + c) * N, :].astype(F32)
        for k in range(K):
            lhs[c, k, :, N:] = (value * wk[k : k + 1]).astype(BF16)
    arrive(VAL, (0, 0), (0, 3))
    for c in range(2):
        gather(c, 0, hc, True)
    arrive(POS, (1, 0), (1, 3))
    for c in range(2):
        weights(c, 1)
    for col in (1, 2):
        arrive(VAL, (1, col))
        send(VAL, RELAY[col])
    arrive(POS, (2, 0), (2, 1), (2, 2), (2, 3))
    for c in range(2):
        weights(c, 2)
    arrive(VAL, (1, 0), (1, 3))
    for c in range(2):
        gather(c, 1, hc, False)
    arrive(VAL, (2, 0), (2, 1), (2, 2), (2, 3))
    for c in range(2):
        gather(c, 2, hc, False)

    pre = []
    halves = []
    for c in range(2):
        total = usum[c, 0] * wk[0:1]
        for k in range(1, K):
            total = total + usum[c, k] * wk[k : k + 1]
        halves.append(total.astype(BF16))
        pre.append(dot(halves[c], w_out[...]))
    grad_pre = []
    sigs = []
    for c in range(2):
        sig = jax.nn.sigmoid(pre[c])
        sigs.append(sig)
        grad_pre.append((cot[0, c].astype(F32) * sig * (1.0 + pre[c] * (1.0 - sig))).astype(BF16))
        hg[0, (1 + c) * N : (2 + c) * N, :] = dot(grad_pre[c], w_out[...], ((1,), (1,))).astype(BF16)
    send(GRAD, FIRST)
    for c in range(2):
        out_feat[0, c] = (feat[0, c].astype(F32) + pre[c] * sigs[c]).astype(BF16)
    wout_part = dot(halves[0], grad_pre[0], ((0,), (0,))) + dot(halves[1], grad_pre[1], ((0,), (0,)))
    grad_agg = [hg[0, (1 + c) * N : (2 + c) * N, :].astype(F32) for c in range(2)]
    rows = []
    for k in range(K):
        rows.append(jnp.sum(grad_agg[0] * usum[0, k] + grad_agg[1] * usum[1, k], axis=0, keepdims=True))
    wradial_part = jnp.concatenate(rows, axis=0) * fold

    def spread(a, main, small):
        for q in range(16):
            extra = jnp.broadcast_to(small[q % small.shape[0] : q % small.shape[0] + 1], (8, N))
            ar_src[a, q] = jnp.concatenate([main[8 * q : 8 * q + 8], extra], axis=0).astype(BF16)
        ar_one[a, pl.ds(q_me, 1)] = ar_src[a, pl.ds(q_me, 1)]

        @pl.loop(1, 16)
        def _(d):
            q = lax.rem(q_me + d, 16)
            pltpu.make_async_remote_copy(
                src_ref=ar_src.at[a, q], dst_ref=ar_one.at[a, q_me],
                send_sem=ar_send.at[a, 0], recv_sem=ar_recv.at[a, 0],
                device_id=group_one(q), device_id_type=MESH,
            ).start()

    def batch(buffer, a, count, phase):
        return pltpu.make_async_remote_copy(
            src_ref=buffer.at[a, pl.ds(0, count)], dst_ref=buffer.at[a, pl.ds(0, count)],
            send_sem=ar_send.at[a, phase], recv_sem=ar_recv.at[a, phase],
            device_id=dev["O"], device_id_type=MESH,
        )

    def middle(a):
        batch(ar_one, a, 15, 0).wait_recv()
        ar_mid[a] = jnp.sum(ar_one[a].astype(F32), axis=0).astype(BF16)
        ar_two[a, pl.ds(p_me, 1)] = ar_mid[a][None]

        @pl.loop(1, 8)
        def _(d):
            pltpu.make_async_remote_copy(
                src_ref=ar_mid.at[a], dst_ref=ar_two.at[a, p_me],
                send_sem=ar_send.at[a, 1], recv_sem=ar_recv.at[a, 1],
                device_id=group_two(lax.rem(p_me + d, 8)), device_id_type=MESH,
            ).start()

    def collect(a):
        batch(ar_two, a, 7, 1).wait_recv()
        final = jnp.sum(ar_two[a].astype(F32), axis=0).astype(BF16)
        ar_three[a, pl.ds(q_me, 1)] = final[None]

        @pl.loop(1, 16)
        def _(d):
            pltpu.make_async_remote_copy(
                src_ref=ar_three.at[a, q_me], dst_ref=ar_three.at[a, q_me],
                send_sem=ar_send.at[a, 2], recv_sem=ar_recv.at[a, 2],
                device_id=group_one(lax.rem(q_me + d, 16)), device_id_type=MESH,
            ).start()

    def finish(a, main, small):
        batch(ar_three, a, 15, 2).wait_recv()
        for q in range(16):
            chunk = ar_three[a, q].astype(F32)
            main[8 * q : 8 * q + 8, :] = chunk[0:8]
            if q < small.shape[0]:
                small[q : q + 1, :] = chunk[8:9]

    spread(0, wout_part, wradial_part)
    for c in range(2):
        for k in range(K):
            lhs[c, k, :, :N] = (grad_agg[c] * wk[k : k + 1]).astype(BF16)
        pacc[c] = jnp.zeros((3, N, N), F32)

    def pulls(c, role):
        both = jnp.concatenate([hc[role, c * N : (c + 3) * N, :], hg[role, c * N : (c + 3) * N, :]], axis=1)
        sbuf[...] = dot(lhs[c].reshape(K * N, 2 * N), both, ((1,), (1,))).reshape(K, N, 3 * N)
        near_rows = near(c, role)

        @pl.loop(0, N // ROWS)
        def _(i):
            i0 = pl.multiple_of(i * ROWS, ROWS)
            deltas, inside, inverse, ratio, base = geometry(c, role, near_rows, i0)
            total = sbuf[K - 1, pl.ds(i0, ROWS), :]
            slope = total
            for k in range(K - 2, -1, -1):
                total = total * ratio + sbuf[k, pl.ds(i0, ROWS), :]
                if k > 0:
                    slope = slope * ratio + total
            slope = slope * ratio
            pull = base * inside * (2.0 * total + GAMMA * inside * (total - slope * inverse * (1.0 / (K - 1.0))))
            for n in range(3):
                part = pull * deltas[n]
                pacc[c, n, pl.ds(i0, ROWS), :] += part[:, :N] + part[:, N : 2 * N] + part[:, 2 * N :]

    arrive(GRAD, (0, 0), (0, 3))
    for c in range(2):
        gather(c, 0, hg, True)
    for c in range(2):
        pulls(c, 0)
    middle(0)
    for col in (1, 2):
        arrive(GRAD, (1, col))
        send(GRAD, RELAY[col])
    collect(0)
    arrive(GRAD, (1, 0), (1, 3))
    for c in range(2):
        gather(c, 1, hg, False)
    for c in range(2):
        pulls(c, 1)
    arrive(GRAD, (2, 0), (2, 1), (2, 2), (2, 3))
    for c in range(2):
        gather(c, 2, hg, False)

    value_part = jnp.zeros((N, N), F32)
    gain_part = jnp.zeros((16, N), F32)
    back = []
    for c in range(2):
        total = usum[c, 0] * wk[0:1]
        for k in range(1, K):
            total = total + usum[c, k] * wk[k : k + 1]
        half = (total * gain[c]).astype(BF16)
        back.append(half)
        value_part = value_part + dot(feat[0, c], half, ((0,), (0,)))
        gain_part = gain_part + dot(onehot[c], total * proj[c], precision=lax.Precision.HIGHEST)
    spread(1, value_part, gain_part)
    pulls(0, 2)
    middle(1)
    pulls(1, 2)
    collect(1)
    for c in range(2):
        change = dot(back[c], w_value[...], ((1,), (1,)))
        grad_feat[0, c] = (cot[0, c].astype(F32) + change).astype(BF16)
        for n in range(3):
            scale = 2.0 * (HZ if n == 2 else 1.0)
            grad_pos[0, c, n : n + 1, :] = jnp.sum(pacc[c, n].T, axis=0, keepdims=True) * scale
    finish(0, grad_wout, grad_wradial)
    finish(1, grad_wvalue, grad_gain)
    for copy in sent:
        copy.wait_send()
    for a in range(2):
        batch(ar_one, a, 15, 0).wait_send()
        batch(ar_two, a, 7, 1).wait_send()
        batch(ar_three, a, 15, 2).wait_send()


def on_device(features, positions, bead_types, cell_counts, w_value, w_radial, type_gain, w_out, cotangent):
    vmem = pl.BlockSpec(memory_space=pltpu.VMEM)
    smem = pl.BlockSpec(memory_space=pltpu.SMEM)
    shape = jax.ShapeDtypeStruct
    return pl.pallas_call(
        kernel,
        out_shape=(
            shape((1, 2, N, N), BF16),
            shape((1, 2, N, N), BF16),
            shape((1, 2, 3, N), F32),
            shape((N, N), F32),
            shape((K, N), F32),
            shape((16, N), F32),
            shape((N, N), F32),
        ),
        in_specs=[vmem, vmem, vmem, smem, vmem, vmem, vmem, vmem, vmem],
        out_specs=(vmem,) * 7,
        scratch_shapes=[
            pltpu.VMEM((3, 8, 4 * N), F32),
            pltpu.VMEM((3, 4 * N, N), BF16),
            pltpu.VMEM((3, 4 * N, N), BF16),
            pltpu.VMEM((2, 3, N, N), F32),
            pltpu.VMEM((2, 3, K, N, 3 * N), BF16),
            pltpu.VMEM((2, K, N, N), F32),
            pltpu.VMEM((K, N, 3 * N), F32),
            pltpu.VMEM((2, K, N, 2 * N), BF16),
            pltpu.VMEM((2, 3, N, N), F32),
            pltpu.VMEM((2, N, N), F32),
            pltpu.VMEM((2, N, N), F32),
            pltpu.VMEM((2, 16, N), F32),
            pltpu.VMEM((2, 16, 16, N), BF16),
            pltpu.VMEM((2, 16, 16, N), BF16),
            pltpu.VMEM((2, 16, N), BF16),
            pltpu.VMEM((2, 8, 16, N), BF16),
            pltpu.VMEM((2, 16, 16, N), BF16),
            pltpu.SemaphoreType.DMA((30,)),
            pltpu.SemaphoreType.DMA((3, 12)),
            pltpu.SemaphoreType.DMA((2, 3)),
            pltpu.SemaphoreType.DMA((2, 3)),
        ],
        compiler_params=pltpu.CompilerParams(
            collective_id=0, has_side_effects=True, vmem_limit_bytes=40 * 1024 * 1024
        ),
        cost_estimate=pl.CostEstimate(flops=3_000_000_000, bytes_accessed=1_000_000, transcendentals=4_000_000),
    )(features, positions, bead_types, cell_counts, w_value, w_radial, type_gain, w_out, cotangent)


def solution(mesh):
    cells = P(("frame", "gx"), "gy", None, None)
    return jax.shard_map(
        on_device,
        mesh=mesh,
        in_specs=(cells, cells, P(("frame", "gx"), "gy", None), P(("frame", "gx"), "gy"), P(), P(), P(), P(), cells),
        out_specs=(cells, cells, cells) + (P("frame", None),) * 4,
        check_vma=False,
    )
```

```python
import jax
import jax.numpy as jnp
from jax import lax
from jax.experimental import pallas as pl
from jax.experimental.pallas import tpu as pltpu
from jax.sharding import PartitionSpec as P

MESH = pl.DeviceIdType.MESH
F32 = jnp.float32
BF16 = jnp.bfloat16
EXACT = lax.Precision.HIGHEST
HZ = 6.0
SOFTEN = 0.01
N = 128
K = 8
NX = 8
NY = 16
GAMMA = 24.5
FAR = 1000.0
POS, VAL, GRAD = 0, 1, 2
ROWS = 16
COMM = True

FIRST = (
    ((0, 1), (1, 1), "O", "all"),
    ((0, 2), (1, 2), "O", "all"),
    ((0, 1), (0, 3), "W", "all"),
    ((0, 2), (0, 0), "E", "all"),
    ((0, 1), (1, 3), "OW", "first"),
    ((0, 1), (2, 3), "RW", "first"),
    ((0, 2), (1, 0), "OE", "last"),
    ((0, 2), (2, 0), "RE", "last"),
)
RELAY = {
    1: (((1, 1), (2, 1), "P", "all"), ((1, 1), (1, 3), "W", "not first"), ((1, 1), (2, 3), "PW", "not first")),
    2: (((1, 2), (2, 2), "P", "all"), ((1, 2), (1, 0), "E", "not last"), ((1, 2), (2, 0), "PE", "not last")),
}


def dot(a, b, dims=((1,), (0,)), precision=None):
    return lax.dot_general(a, b, (dims, ((), ())), precision=precision, preferred_element_type=F32)


def kernel(
    feat_in, pos_in, types_in, counts_in, w_value_in, w_radial_in, type_gain_in, w_out_in, cot_in,
    out_feat, grad_feat, grad_pos, grad_wvalue, grad_wradial, grad_gain, grad_wout,
    hp, hf, hc, hg, own, ebuf, geo, usum, sbuf, lhs, pacc, proj, gain, onehot, wkt, sct, vt,
    pos, types, counts, w_value, w_radial, type_gain, w_out, cot,
    ar_src, ar_one, ar_mid, ar_two, ar_three,
    load_sem, send_sem, recv_sem, ar_send, ar_recv,
):
    gx = lax.axis_index("gx")
    gy = lax.axis_index("gy")
    zh = lax.rem(gx, 2)
    yy = gx // 2
    side = 1 - 2 * zh
    side_f = side.astype(F32)
    west, east = lax.rem(gy + NY - 1, NY), lax.rem(gy + 1, NY)
    across = lax.rem(gx + side + NX, NX)
    other = lax.rem(gx - side + NX, NX)
    beyond = lax.rem(gx + 2 * side + NX, NX)
    behind = lax.rem(gx - 2 * side + NX, NX)
    dev = {
        "O": (across, gy), "OW": (across, west), "OE": (across, east),
        "RW": (other, west), "RE": (other, east),
        "W": (gx, west), "E": (gx, east),
        "P": (beyond, gy), "PW": (beyond, west), "PE": (beyond, east),
        "Q": (behind, gy), "QW": (behind, west), "QE": (behind, east),
    }
    dev = {name: {"gx": x, "gy": y} for name, (x, y) in dev.items()}
    quad = gy // 4
    q_me = yy * 4 + lax.rem(gy, 4)
    p_me = zh * 4 + quad

    def group_one(q):
        return {"gx": 2 * (q // 4) + zh, "gy": quad * 4 + lax.rem(q, 4)}

    def group_two(p):
        return {"gx": 2 * yy + p // 4, "gy": lax.rem(p, 4) * 4 + lax.rem(gy, 4)}

    barrier = pltpu.get_barrier_semaphore()
    if COMM:
        for name in dev:
            pl.semaphore_signal(barrier, inc=1, device_id=dev[name], device_id_type=MESH)

        @pl.loop(1, 16)
        def _(d):
            pl.semaphore_signal(barrier, inc=1, device_id=group_one(lax.rem(q_me + d, 16)), device_id_type=MESH)

        @pl.loop(1, 8)
        def _(d):
            pl.semaphore_signal(barrier, inc=1, device_id=group_two(lax.rem(p_me + d, 8)), device_id_type=MESH)

    loads = []
    for n, (src, dst) in enumerate((
        (pos_in, pos), (types_in, types), (counts_in, counts), (w_radial_in, w_radial),
        (feat_in.at[0, 0], hf.at[0, N : 2 * N, :]), (feat_in.at[0, 1], hf.at[0, 2 * N : 3 * N, :]),
        (type_gain_in, type_gain), (w_value_in, w_value), (w_out_in, w_out), (cot_in, cot),
    )):
        loads.append(pltpu.make_async_copy(src, dst, load_sem.at[n]))
        loads[-1].start()

    for load in loads[:4]:
        load.wait()
    lane = lax.broadcasted_iota(jnp.int32, (1, N), 1)
    for c in range(2):
        missing = jnp.where(lane < counts[:, c : c + 1], 0.0, FAR)
        x, y, z = (pos[0, n, c : c + 1, :] for n in range(3))
        z = z * HZ
        kind = types[0, c : c + 1, :].astype(F32)
        hp[0, :, (1 + c) * N : (2 + c) * N] = jnp.concatenate(
            [x, y, z + missing, kind, jnp.zeros((4, N), F32)], axis=0
        )
        for n, row in enumerate((x, y, z - missing)):
            own[c, n] = jnp.broadcast_to(row, (N, N)).T
    basis = lax.broadcasted_iota(jnp.int32, (K, N), 0).astype(F32)
    fold = jnp.exp(-0.5 * basis * basis)
    wk = w_radial[...] * fold
    for k in range(K):
        wkt[k] = jnp.broadcast_to(wk[k : k + 1], (N, N)).T
    for load in loads[4:]:
        load.wait()

    def slot(kind, place):
        role, column = place
        if kind == POS:
            return hp.at[role, :, column * N : (column + 1) * N]
        return (hf if kind == VAL else hg).at[role, column * N : (column + 1) * N, :]

    sent = []

    def where_sent(who, act):
        if who == "all":
            act()
        else:
            pl.when({
                "first": gy == 0, "not first": gy != 0, "last": gy == NY - 1, "not last": gy != NY - 1
            }[who])(act)

    def send(kind, messages):
        if not COMM:
            return
        for src, dst, to, who in messages:
            copy = pltpu.make_async_remote_copy(
                src_ref=slot(kind, src),
                dst_ref=slot(kind, dst),
                send_sem=send_sem.at[len(sent)],
                recv_sem=recv_sem.at[kind, dst[0] * 4 + dst[1]],
                device_id=dev[to],
                device_id_type=MESH,
            )
            where_sent(who, copy.start)
            sent.append((who, copy))

    def arrive(kind, *places):
        if not COMM:
            return
        for place in places:
            pltpu.make_async_remote_copy(
                src_ref=slot(kind, place),
                dst_ref=slot(kind, place),
                send_sem=send_sem.at[0],
                recv_sem=recv_sem.at[kind, place[0] * 4 + place[1]],
                device_id=dev["O"],
                device_id_type=MESH,
            ).wait_recv()

    if COMM:
        pl.semaphore_wait(barrier, len(dev) + 15 + 7)
    send(POS, FIRST)
    send(VAL, FIRST)

    window = lax.broadcasted_iota(jnp.int32, (1, 3 * N), 1)
    shift_y = (window // N - 1).astype(F32)

    def near(c, role):
        block = hp[role, :, c * N : (c + 3) * N]
        shift_x = (0.0, side_f, -side_f)[role]
        return block[0:1] + shift_x, block[1:2] + shift_y, block[2:3]

    def deltas_of(c, near_rows, i0):
        deltas = []
        for n in range(3):
            mine = own[c, n, pl.ds(i0, ROWS), :]
            deltas.append(near_rows[n] - jnp.concatenate([mine] * 3, axis=1))
        return deltas

    def weights(c, role):
        near_rows = near(c, role)

        @pl.loop(0, N // ROWS)
        def _(i):
            i0 = pl.multiple_of(i * ROWS, ROWS)
            dx, dy, dz = deltas_of(c, near_rows, i0)
            dist = dx * dx + dy * dy + dz * dz
            if role == 0:
                row = lax.broadcasted_iota(jnp.int32, (ROWS, 3 * N), 0) + (i0 + N)
                col = lax.broadcasted_iota(jnp.int32, (ROWS, 3 * N), 1)
                dist = jnp.where(row == col, 2.0, dist)
            inside = jnp.maximum(1.0 - dist, 0.0)
            soft = (1.0 + SOFTEN) - inside
            inverse = lax.rsqrt(soft)
            ratio = jnp.exp((K - 1.0) * (soft * inverse))
            lead = inside * jnp.exp(-GAMMA * soft)
            value = inside * lead
            geo[c, role, 0, pl.ds(i0, ROWS), :] = ratio
            geo[c, role, 1, pl.ds(i0, ROWS), :] = 2.0 * lead + GAMMA * value
            geo[c, role, 2, pl.ds(i0, ROWS), :] = value * inverse * (GAMMA / (K - 1.0))
            for k in range(K):
                ebuf[c, role, k, pl.ds(i0, ROWS), :] = value.astype(BF16)
                if k < K - 1:
                    value = value * ratio

    def gather(c, role, table, first):
        got = dot(ebuf[c, role].reshape(K * N, 3 * N), table[role, c * N : (c + 3) * N, :]).reshape(K, N, N)
        if first:
            usum[c] = got
        else:
            usum[c] += got

    kind_of = lax.broadcasted_iota(jnp.int32, (16, 4 * N), 0).astype(F32)

    def gains(role):
        hot = jnp.where(kind_of == hp[role, 3:4, :], 1.0, 0.0)
        onehot[role] = hot
        gain[role] = dot(hot, type_gain[...], ((0,), (0,)), EXACT)

    def values(role):
        projected = dot(hf[role], w_value[...])
        proj[role] = projected
        hc[role] = (projected * gain[role]).astype(BF16)

    arrive(POS, (0, 0), (0, 3))
    for c in range(2):
        weights(c, 0)
    gains(0)
    for col in (1, 2):
        arrive(POS, (1, col))
        send(POS, RELAY[col])
    arrive(VAL, (0, 0), (0, 3))
    values(0)
    for c in range(2):
        gather(c, 0, hc, True)
    for col in (1, 2):
        arrive(VAL, (1, col))
        send(VAL, RELAY[col])
    for c in range(2):
        value = hc[0, (1 + c) * N : (2 + c) * N, :].astype(F32)
        for k in range(K):
            lhs[c, k, :, N:] = (value * wk[k : k + 1]).astype(BF16)
    arrive(POS, (1, 0), (1, 3))
    for c in range(2):
        weights(c, 1)
    gains(1)
    arrive(POS, (2, 0), (2, 1), (2, 2), (2, 3))
    for c in range(2):
        weights(c, 2)
    gains(2)
    arrive(VAL, (1, 0), (1, 3))
    values(1)
    for c in range(2):
        gather(c, 1, hc, False)
    arrive(VAL, (2, 0), (2, 1), (2, 2), (2, 3))
    values(2)
    for c in range(2):
        gather(c, 2, hc, False)

    def own_rows(c):
        return slice((1 + c) * N, (2 + c) * N)

    pre = []
    halves = []
    for c in range(2):
        total = usum[c, 0] * wk[0:1]
        for k in range(1, K):
            total = total + usum[c, k] * wk[k : k + 1]
        halves.append(total.astype(BF16))
        pre.append(dot(halves[c], w_out[...]))
    grad_pre = []
    sigs = []
    grad_agg = []
    for c in range(2):
        sig = jax.nn.sigmoid(pre[c])
        sigs.append(sig)
        grad_pre.append((cot[0, c].astype(F32) * sig * (1.0 + pre[c] * (1.0 - sig))).astype(BF16))
        half = dot(grad_pre[c], w_out[...], ((1,), (1,))).astype(BF16)
        hg[0, own_rows(c), :] = half
        grad_agg.append(half.astype(F32))
    send(GRAD, FIRST)

    for c in range(2):
        flipped = grad_agg[c].T
        for k in range(K):
            sct[c, :, k * N : (k + 1) * N] = (flipped * wkt[k]).astype(BF16)
    for role in range(3):
        vt[role, :, 3 * N :] = jnp.zeros((N, N), F32)
        vt[role, :, : 3 * N] = dot(sct[0], ebuf[0, role].reshape(K * N, 3 * N))
        vt[role, :, N:] += dot(sct[1], ebuf[1, role].reshape(K * N, 3 * N))
    value_part = jnp.zeros((N, N), F32)
    gain_part = jnp.zeros((16, N), F32)
    for role in range(3):
        given = vt[role].T
        half = (given * gain[role]).astype(BF16)
        value_part = value_part + dot(hf[role], half, ((0,), (0,)))
        gain_part = gain_part + dot(onehot[role], given * proj[role], precision=EXACT)
    wout_part = dot(halves[0], grad_pre[0], ((0,), (0,))) + dot(halves[1], grad_pre[1], ((0,), (0,)))
    rows = []
    for k in range(K):
        rows.append(jnp.sum(grad_agg[0] * usum[0, k] + grad_agg[1] * usum[1, k], axis=0, keepdims=True))
    wradial_part = jnp.concatenate(rows, axis=0) * fold

    for q in range(16):
        own_q = slice(8 * q, 8 * q + 8)
        ar_src[q] = jnp.concatenate(
            [
                value_part[own_q],
                wout_part[own_q],
                jnp.broadcast_to(gain_part[q : q + 1], (8, N)),
                jnp.broadcast_to(wradial_part[q % K : q % K + 1], (8, N)),
            ],
            axis=0,
        ).astype(BF16)
    ar_one[pl.ds(q_me, 1)] = ar_src[pl.ds(q_me, 1)]

    def batch(buffer, count, phase):
        return pltpu.make_async_remote_copy(
            src_ref=buffer.at[pl.ds(0, count)], dst_ref=buffer.at[pl.ds(0, count)],
            send_sem=ar_send.at[phase], recv_sem=ar_recv.at[phase],
            device_id=dev["O"], device_id_type=MESH,
        )

    if COMM:
        @pl.loop(1, 16)
        def _(d):
            q = lax.rem(q_me + d, 16)
            pltpu.make_async_remote_copy(
                src_ref=ar_src.at[q], dst_ref=ar_one.at[q_me],
                send_sem=ar_send.at[0], recv_sem=ar_recv.at[0],
                device_id=group_one(q), device_id_type=MESH,
            ).start()

    def middle():
        if COMM:
            batch(ar_one, 15, 0).wait_recv()
        ar_mid[...] = jnp.sum(ar_one[...].astype(F32), axis=0).astype(BF16)
        ar_two[pl.ds(p_me, 1)] = ar_mid[...][None]
        if COMM:
            @pl.loop(1, 8)
            def _(d):
                pltpu.make_async_remote_copy(
                    src_ref=ar_mid, dst_ref=ar_two.at[p_me],
                    send_sem=ar_send.at[1], recv_sem=ar_recv.at[1],
                    device_id=group_two(lax.rem(p_me + d, 8)), device_id_type=MESH,
                ).start()

    def collect():
        if COMM:
            batch(ar_two, 7, 1).wait_recv()
        final = jnp.sum(ar_two[...].astype(F32), axis=0).astype(BF16)
        ar_three[pl.ds(q_me, 1)] = final[None]
        if COMM:
            @pl.loop(1, 16)
            def _(d):
                pltpu.make_async_remote_copy(
                    src_ref=ar_three.at[q_me], dst_ref=ar_three.at[q_me],
                    send_sem=ar_send.at[2], recv_sem=ar_recv.at[2],
                    device_id=group_one(lax.rem(q_me + d, 16)), device_id_type=MESH,
                ).start()

    def finish():
        if COMM:
            batch(ar_three, 15, 2).wait_recv()
        for q in range(16):
            chunk = ar_three[q].astype(F32)
            grad_wvalue[8 * q : 8 * q + 8, :] = chunk[0:8]
            grad_wout[8 * q : 8 * q + 8, :] = chunk[8:16]
            grad_gain[q : q + 1, :] = chunk[16:17]
            if q < K:
                grad_wradial[q : q + 1, :] = chunk[24:25]

    for c in range(2):
        for k in range(K):
            lhs[c, k, :, :N] = (grad_agg[c] * wk[k : k + 1]).astype(BF16)
        pacc[c] = jnp.zeros((3, N, N), F32)

    def pulls(c, role):
        span = slice(c * N, (c + 3) * N)
        both = jnp.concatenate([hc[role, span, :], hg[role, span, :]], axis=1)
        sbuf[...] = dot(lhs[c].reshape(K * N, 2 * N), both, ((1,), (1,))).reshape(K, N, 3 * N)
        near_rows = near(c, role)

        @pl.loop(0, N // ROWS)
        def _(i):
            i0 = pl.multiple_of(i * ROWS, ROWS)
            deltas = deltas_of(c, near_rows, i0)
            ratio = geo[c, role, 0, pl.ds(i0, ROWS), :]
            total = sbuf[K - 1, pl.ds(i0, ROWS), :]
            slope = total
            for k in range(K - 2, -1, -1):
                total = total * ratio + sbuf[k, pl.ds(i0, ROWS), :]
                if k > 0:
                    slope = slope * ratio + total
            slope = slope * ratio
            pull = geo[c, role, 1, pl.ds(i0, ROWS), :] * total - geo[c, role, 2, pl.ds(i0, ROWS), :] * slope
            for n in range(3):
                part = pull * deltas[n]
                pacc[c, n, pl.ds(i0, ROWS), :] += part[:, :N] + part[:, N : 2 * N] + part[:, 2 * N :]

    for c in range(2):
        out_feat[0, c] = (hf[0, own_rows(c), :].astype(F32) + pre[c] * sigs[c]).astype(BF16)
    arrive(GRAD, (0, 0), (0, 3))
    for c in range(2):
        gather(c, 0, hg, True)
    middle()
    for col in (1, 2):
        arrive(GRAD, (1, col))
        send(GRAD, RELAY[col])
    for c in range(2):
        pulls(c, 0)
    collect()
    arrive(GRAD, (1, 0), (1, 3))
    for c in range(2):
        gather(c, 1, hg, False)
    for c in range(2):
        pulls(c, 1)
    arrive(GRAD, (2, 0), (2, 1), (2, 2), (2, 3))
    for c in range(2):
        gather(c, 2, hg, False)
    for c in range(2):
        pulls(c, 2)

    for c in range(2):
        total = usum[c, 0] * wk[0:1]
        for k in range(1, K):
            total = total + usum[c, k] * wk[k : k + 1]
        back = (total * gain[0, own_rows(c), :]).astype(BF16)
        change = dot(back, w_value[...], ((1,), (1,)))
        grad_feat[0, c] = (cot[0, c].astype(F32) + change).astype(BF16)
        for n in range(3):
            scale = 2.0 * (HZ if n == 2 else 1.0)
            grad_pos[0, n, c : c + 1, :] = jnp.sum(pacc[c, n].T, axis=0, keepdims=True) * scale
    finish()
    if COMM:
        for who, copy in sent:
            where_sent(who, copy.wait_send)
        batch(ar_one, 15, 0).wait_send()
        batch(ar_two, 7, 1).wait_send()
        batch(ar_three, 15, 2).wait_send()


def store(*refs):
    count = len(refs) // 2
    sems = refs[-1]
    copies = [pltpu.make_async_copy(refs[n], refs[count + n], sems.at[n]) for n in range(count)]
    for copy in copies:
        copy.start()
    for copy in copies:
        copy.wait()


def on_device(features, positions, bead_types, cell_counts, w_value, w_radial, type_gain, w_out, cotangent):
    vmem = pl.BlockSpec(memory_space=pltpu.VMEM)
    anywhere = pl.BlockSpec(memory_space=pl.ANY)
    shape = jax.ShapeDtypeStruct
    shapes = (
        shape((1, 2, N, N), BF16),
        shape((1, 2, N, N), BF16),
        shape((1, 3, 2, N), F32),
        shape((N, N), F32),
        shape((K, N), F32),
        shape((16, N), F32),
        shape((N, N), F32),
    )
    results = pl.pallas_call(
        kernel,
        out_shape=shapes,
        in_specs=[pl.BlockSpec(memory_space=pltpu.HBM)] * 9,
        out_specs=(vmem,) * 7,
        scratch_shapes=[
            pltpu.VMEM((3, 8, 4 * N), F32),
            pltpu.VMEM((3, 4 * N, N), BF16),
            pltpu.VMEM((3, 4 * N, N), BF16),
            pltpu.VMEM((3, 4 * N, N), BF16),
            pltpu.VMEM((2, 3, N, N), F32),
            pltpu.VMEM((2, 3, K, N, 3 * N), BF16),
            pltpu.VMEM((2, 3, 3, N, 3 * N), F32),
            pltpu.VMEM((2, K, N, N), F32),
            pltpu.VMEM((K, N, 3 * N), F32),
            pltpu.VMEM((2, K, N, 2 * N), BF16),
            pltpu.VMEM((2, 3, N, N), F32),
            pltpu.VMEM((3, 4 * N, N), F32),
            pltpu.VMEM((3, 4 * N, N), F32),
            pltpu.VMEM((3, 16, 4 * N), F32),
            pltpu.VMEM((K, N, N), F32),
            pltpu.VMEM((2, N, K * N), BF16),
            pltpu.VMEM((3, N, 4 * N), F32),
            pltpu.VMEM((1, 3, 2, N), F32),
            pltpu.VMEM((1, 2, N), jnp.int32),
            pltpu.VMEM((1, 2), jnp.int32),
            pltpu.VMEM((N, N), BF16),
            pltpu.VMEM((K, N), F32),
            pltpu.VMEM((16, N), F32),
            pltpu.VMEM((N, N), BF16),
            pltpu.VMEM((1, 2, N, N), BF16),
            pltpu.VMEM((16, 32, N), BF16),
            pltpu.VMEM((16, 32, N), BF16),
            pltpu.VMEM((32, N), BF16),
            pltpu.VMEM((8, 32, N), BF16),
            pltpu.VMEM((16, 32, N), BF16),
            pltpu.SemaphoreType.DMA((10,)),
            pltpu.SemaphoreType.DMA((42,)),
            pltpu.SemaphoreType.DMA((3, 12)),
            pltpu.SemaphoreType.DMA((3,)),
            pltpu.SemaphoreType.DMA((3,)),
        ],
        compiler_params=pltpu.CompilerParams(
            collective_id=0, has_side_effects=True, vmem_limit_bytes=60 * 1024 * 1024
        ),
        cost_estimate=pl.CostEstimate(flops=4_000_000_000, bytes_accessed=1_000_000, transcendentals=4_000_000),
    )(features, positions.transpose(0, 2, 1, 3), bead_types, cell_counts, w_value, w_radial, type_gain, w_out, cotangent)
    out = pl.pallas_call(
        store,
        out_shape=shapes,
        in_specs=[anywhere] * 7,
        out_specs=(pl.BlockSpec(memory_space=pltpu.HBM),) * 7,
        scratch_shapes=[pltpu.SemaphoreType.DMA((7,))],
        compiler_params=pltpu.CompilerParams(vmem_limit_bytes=60 * 1024 * 1024),
    )(*results)
    return (out[0], out[1], out[2].transpose(0, 2, 1, 3)) + tuple(out[3:])


def solution(mesh):
    cells = P(("frame", "gx"), "gy", None, None)
    return jax.shard_map(
        on_device,
        mesh=mesh,
        in_specs=(cells, cells, P(("frame", "gx"), "gy", None), P(("frame", "gx"), "gy"), P(), P(), P(), P(), cells),
        out_specs=(cells, cells, cells) + (P("frame", None),) * 4,
        check_vma=False,
    )
```

```python
import jax
import jax.numpy as jnp
from jax import lax
from jax.experimental import pallas as pl
from jax.experimental.pallas import tpu as pltpu
from jax.sharding import PartitionSpec as P

MESH = pl.DeviceIdType.MESH
F32 = jnp.float32
BF16 = jnp.bfloat16
EXACT = lax.Precision.HIGHEST
HZ = 6.0
SOFTEN = 0.01
N = 128
K = 8
NX = 8
NY = 16
GAMMA = 24.5
FAR = 1000.0
POS, VAL, GRAD = 0, 1, 2
ROWS = 16
COMM = True

FIRST = (
    ((0, 1), (1, 1), "O", "all"),
    ((0, 2), (1, 2), "O", "all"),
    ((0, 1), (0, 3), "W", "all"),
    ((0, 2), (0, 0), "E", "all"),
    ((0, 1), (1, 3), "OW", "first"),
    ((0, 1), (2, 3), "RW", "first"),
    ((0, 2), (1, 0), "OE", "last"),
    ((0, 2), (2, 0), "RE", "last"),
)
RELAY = {
    1: (((1, 1), (2, 1), "P", "all"), ((1, 1), (1, 3), "W", "not first"), ((1, 1), (2, 3), "PW", "not first")),
    2: (((1, 2), (2, 2), "P", "all"), ((1, 2), (1, 0), "E", "not last"), ((1, 2), (2, 0), "PE", "not last")),
}


def dot(a, b, dims=((1,), (0,)), precision=None):
    return lax.dot_general(a, b, (dims, ((), ())), precision=precision, preferred_element_type=F32)


def kernel(
    feat_in, pos_in, types_in, counts_in, w_value_in, w_radial_in, type_gain_in, w_out_in, cot_in,
    out_feat, grad_feat, grad_pos, grad_wvalue, grad_wradial, grad_gain, grad_wout,
    hp, hf, hc, hg, own, ebuf, geo, usum, sbuf, lhs, pacc, proj, gain, onehot, wkt, sct, vt,
    pos, types, counts, w_value, w_radial, type_gain, w_out, cot,
    ar_src, ar_one, ar_mid, ar_two, ar_three,
    load_sem, send_sem, recv_sem, ar_send, ar_recv,
):
    gx = lax.axis_index("gx")
    gy = lax.axis_index("gy")
    zh = lax.rem(gx, 2)
    yy = gx // 2
    side = 1 - 2 * zh
    side_f = side.astype(F32)
    west, east = lax.rem(gy + NY - 1, NY), lax.rem(gy + 1, NY)
    across = lax.rem(gx + side + NX, NX)
    other = lax.rem(gx - side + NX, NX)
    beyond = lax.rem(gx + 2 * side + NX, NX)
    behind = lax.rem(gx - 2 * side + NX, NX)
    dev = {
        "O": (across, gy), "OW": (across, west), "OE": (across, east),
        "RW": (other, west), "RE": (other, east),
        "W": (gx, west), "E": (gx, east),
        "P": (beyond, gy), "PW": (beyond, west), "PE": (beyond, east),
        "Q": (behind, gy), "QW": (behind, west), "QE": (behind, east),
    }
    dev = {name: {"gx": x, "gy": y} for name, (x, y) in dev.items()}
    quad = gy // 4
    q_me = yy * 4 + lax.rem(gy, 4)
    p_me = zh * 4 + quad

    def group_one(q):
        return {"gx": 2 * (q // 4) + zh, "gy": quad * 4 + lax.rem(q, 4)}

    def group_two(p):
        return {"gx": 2 * yy + p // 4, "gy": lax.rem(p, 4) * 4 + lax.rem(gy, 4)}

    loads = [
        pltpu.make_async_copy(src, dst, load_sem.at[n])
        for n, (src, dst) in enumerate((
            (pos_in, pos), (types_in, types), (counts_in, counts), (w_radial_in, w_radial),
            (feat_in.at[0, 0], hf.at[0, N : 2 * N, :]), (feat_in.at[0, 1], hf.at[0, 2 * N : 3 * N, :]),
            (type_gain_in, type_gain), (w_value_in, w_value), (w_out_in, w_out), (cot_in, cot),
        ))
    ]
    for load in loads[:3]:
        load.start()
    barrier = pltpu.get_barrier_semaphore()
    if COMM:
        for name in dev:
            pl.semaphore_signal(barrier, inc=1, device_id=dev[name], device_id_type=MESH)
        for d in range(1, 16):
            pl.semaphore_signal(barrier, inc=1, device_id=group_one(lax.rem(q_me + d, 16)), device_id_type=MESH)
        for d in range(1, 8):
            pl.semaphore_signal(barrier, inc=1, device_id=group_two(lax.rem(p_me + d, 8)), device_id_type=MESH)
    for load in loads[3:]:
        load.start()

    for load in loads[:3]:
        load.wait()
    lane = lax.broadcasted_iota(jnp.int32, (1, N), 1)
    near_z = []
    for c in range(2):
        missing = jnp.where(lane < counts[:, c : c + 1], 0.0, FAR)
        x, y, z = (pos[0, n, c : c + 1, :] for n in range(3))
        z = z * HZ
        kind = types[0, c : c + 1, :].astype(F32)
        near_z.append(z - missing)
        hp[0, :, (1 + c) * N : (2 + c) * N] = jnp.concatenate(
            [x, y, z + missing, kind, jnp.zeros((4, N), F32)], axis=0
        )

    def slot(kind, place, source=False):
        role, column = place
        if kind == VAL and role == 0 and column in (1, 2) and source:
            return feat_in.at[0, column - 1]
        if kind == POS:
            return hp.at[role, :, column * N : (column + 1) * N]
        return (hf if kind == VAL else hg).at[role, column * N : (column + 1) * N, :]

    sent = []

    def where_sent(who, act):
        if who == "all":
            act()
        else:
            pl.when({
                "first": gy == 0, "not first": gy != 0, "last": gy == NY - 1, "not last": gy != NY - 1
            }[who])(act)

    def send(kind, messages):
        if not COMM:
            return
        for src, dst, to, who in messages:
            copy = pltpu.make_async_remote_copy(
                src_ref=slot(kind, src, True),
                dst_ref=slot(kind, dst),
                send_sem=send_sem.at[len(sent)],
                recv_sem=recv_sem.at[kind, dst[0] * 4 + dst[1]],
                device_id=dev[to],
                device_id_type=MESH,
            )
            where_sent(who, copy.start)
            sent.append((who, copy))

    def arrive(kind, *places):
        if not COMM:
            return
        for place in places:
            pltpu.make_async_remote_copy(
                src_ref=slot(kind, place),
                dst_ref=slot(kind, place),
                send_sem=send_sem.at[0],
                recv_sem=recv_sem.at[kind, place[0] * 4 + place[1]],
                device_id=dev["O"],
                device_id_type=MESH,
            ).wait_recv()

    if COMM:
        pl.semaphore_wait(barrier, len(dev) + 15 + 7)
    send(POS, FIRST)
    send(VAL, FIRST)

    for load in loads[3:]:
        load.wait()
    for c in range(2):
        for n, row in enumerate((pos[0, 0, c : c + 1, :], pos[0, 1, c : c + 1, :], near_z[c])):
            own[c, n] = jnp.broadcast_to(row, (N, N)).T
    basis = lax.broadcasted_iota(jnp.int32, (K, N), 0).astype(F32)
    fold = jnp.exp(-0.5 * basis * basis)
    wk = w_radial[...] * fold
    for k in range(K):
        wkt[k] = jnp.broadcast_to(wk[k : k + 1], (N, N)).T

    window = lax.broadcasted_iota(jnp.int32, (1, 3 * N), 1)
    shift_y = (window // N - 1).astype(F32)

    def near(c, role):
        block = hp[role, :, c * N : (c + 3) * N]
        shift_x = (0.0, side_f, -side_f)[role]
        return block[0:1] + shift_x, block[1:2] + shift_y, block[2:3]

    def deltas_of(c, near_rows, i0):
        deltas = []
        for n in range(3):
            mine = own[c, n, pl.ds(i0, ROWS), :]
            deltas.append(near_rows[n] - jnp.concatenate([mine] * 3, axis=1))
        return deltas

    def weights(c, role):
        near_rows = near(c, role)

        @pl.loop(0, N // ROWS)
        def _(i):
            i0 = pl.multiple_of(i * ROWS, ROWS)
            dx, dy, dz = deltas_of(c, near_rows, i0)
            dist = dx * dx + dy * dy + dz * dz
            if role == 0:
                row = lax.broadcasted_iota(jnp.int32, (ROWS, 3 * N), 0) + (i0 + N)
                col = lax.broadcasted_iota(jnp.int32, (ROWS, 3 * N), 1)
                dist = jnp.where(row == col, 2.0, dist)
            inside = jnp.maximum(1.0 - dist, 0.0)
            soft = (1.0 + SOFTEN) - inside
            inverse = lax.rsqrt(soft)
            ratio = jnp.exp((K - 1.0) * (soft * inverse))
            lead = inside * jnp.exp(-GAMMA * soft)
            value = inside * lead
            geo[c, role, 0, pl.ds(i0, ROWS), :] = ratio
            geo[c, role, 1, pl.ds(i0, ROWS), :] = 2.0 * lead + GAMMA * value
            geo[c, role, 2, pl.ds(i0, ROWS), :] = value * inverse * (GAMMA / (K - 1.0))
            for k in range(K):
                ebuf[c, role, k, pl.ds(i0, ROWS), :] = value.astype(BF16)
                if k < K - 1:
                    value = value * ratio

    def gather(c, role, table, first):
        got = dot(ebuf[c, role].reshape(K * N, 3 * N), table[role, c * N : (c + 3) * N, :]).reshape(K, N, N)
        if first:
            usum[c] = got
        else:
            usum[c] += got

    kind_of = lax.broadcasted_iota(jnp.int32, (16, 4 * N), 0).astype(F32)

    def gains(role):
        hot = jnp.where(kind_of == hp[role, 3:4, :], 1.0, 0.0)
        onehot[role] = hot
        gain[role] = dot(hot, type_gain[...], ((0,), (0,)), EXACT)

    def values(role):
        projected = dot(hf[role], w_value[...])
        proj[role] = projected
        hc[role] = (projected * gain[role]).astype(BF16)

    arrive(POS, (0, 0), (0, 3))
    for c in range(2):
        weights(c, 0)
    gains(0)
    for col in (1, 2):
        arrive(POS, (1, col))
        send(POS, RELAY[col])
    arrive(VAL, (0, 0), (0, 3))
    values(0)
    for c in range(2):
        gather(c, 0, hc, True)
    for col in (1, 2):
        arrive(VAL, (1, col))
        send(VAL, RELAY[col])
    for c in range(2):
        value = hc[0, (1 + c) * N : (2 + c) * N, :].astype(F32)
        for k in range(K):
            lhs[c, k, :, N:] = (value * wk[k : k + 1]).astype(BF16)
    arrive(POS, (1, 0), (1, 3))
    for c in range(2):
        weights(c, 1)
    gains(1)
    arrive(POS, (2, 0), (2, 1), (2, 2), (2, 3))
    for c in range(2):
        weights(c, 2)
    gains(2)
    arrive(VAL, (1, 0), (1, 3))
    values(1)
    for c in range(2):
        gather(c, 1, hc, False)
    arrive(VAL, (2, 0), (2, 1), (2, 2), (2, 3))
    values(2)

    def own_rows(c):
        return slice((1 + c) * N, (2 + c) * N)

    pre = []
    halves = []
    grad_pre = []
    sigs = []
    grad_agg = []
    for c in range(2):
        gather(c, 2, hc, False)
        total = usum[c, 0] * wk[0:1]
        for k in range(1, K):
            total = total + usum[c, k] * wk[k : k + 1]
        halves.append(total.astype(BF16))
        pre.append(dot(halves[c], w_out[...]))
        sig = jax.nn.sigmoid(pre[c])
        sigs.append(sig)
        grad_pre.append((cot[0, c].astype(F32) * sig * (1.0 + pre[c] * (1.0 - sig))).astype(BF16))
        half = dot(grad_pre[c], w_out[...], ((1,), (1,))).astype(BF16)
        hg[0, own_rows(c), :] = half
        grad_agg.append(half.astype(F32))
        send(GRAD, [message for message in FIRST if message[0] == (0, 1 + c)])

    for c in range(2):
        flipped = grad_agg[c].T
        for k in range(K):
            sct[c, :, k * N : (k + 1) * N] = (flipped * wkt[k]).astype(BF16)
    for role in range(3):
        vt[role, :, 3 * N :] = jnp.zeros((N, N), F32)
        vt[role, :, : 3 * N] = dot(sct[0], ebuf[0, role].reshape(K * N, 3 * N))
        vt[role, :, N:] += dot(sct[1], ebuf[1, role].reshape(K * N, 3 * N))
    value_part = jnp.zeros((N, N), F32)
    gain_part = jnp.zeros((16, N), F32)
    for role in range(3):
        given = vt[role].T
        half = (given * gain[role]).astype(BF16)
        value_part = value_part + dot(hf[role], half, ((0,), (0,)))
        gain_part = gain_part + dot(onehot[role], given * proj[role], precision=EXACT)
    wout_part = dot(halves[0], grad_pre[0], ((0,), (0,))) + dot(halves[1], grad_pre[1], ((0,), (0,)))
    rows = []
    for k in range(K):
        rows.append(jnp.sum(grad_agg[0] * usum[0, k] + grad_agg[1] * usum[1, k], axis=0, keepdims=True))
    wradial_part = jnp.concatenate(rows, axis=0) * fold

    for q in range(16):
        own_q = slice(8 * q, 8 * q + 8)
        ar_src[q] = jnp.concatenate(
            [
                value_part[own_q],
                wout_part[own_q],
                jnp.broadcast_to(gain_part[q : q + 1], (8, N)),
                jnp.broadcast_to(wradial_part[q % K : q % K + 1], (8, N)),
            ],
            axis=0,
        ).astype(BF16)
    ar_one[pl.ds(q_me, 1)] = ar_src[pl.ds(q_me, 1)]

    def batch(buffer, count, phase):
        return pltpu.make_async_remote_copy(
            src_ref=buffer.at[pl.ds(0, count)], dst_ref=buffer.at[pl.ds(0, count)],
            send_sem=ar_send.at[phase], recv_sem=ar_recv.at[phase],
            device_id=dev["O"], device_id_type=MESH,
        )

    if COMM:
        for d in range(1, 16):
            q = lax.rem(q_me + d, 16)
            pltpu.make_async_remote_copy(
                src_ref=ar_src.at[q], dst_ref=ar_one.at[q_me],
                send_sem=ar_send.at[0], recv_sem=ar_recv.at[0],
                device_id=group_one(q), device_id_type=MESH,
            ).start()

    def middle():
        if COMM:
            batch(ar_one, 15, 0).wait_recv()
        ar_mid[...] = jnp.sum(ar_one[...].astype(F32), axis=0).astype(BF16)
        ar_two[pl.ds(p_me, 1)] = ar_mid[...][None]
        if COMM:
            for d in range(1, 8):
                pltpu.make_async_remote_copy(
                    src_ref=ar_mid, dst_ref=ar_two.at[p_me],
                    send_sem=ar_send.at[1], recv_sem=ar_recv.at[1],
                    device_id=group_two(lax.rem(p_me + d, 8)), device_id_type=MESH,
                ).start()

    def collect():
        if COMM:
            batch(ar_two, 7, 1).wait_recv()
        final = jnp.sum(ar_two[...].astype(F32), axis=0).astype(BF16)
        ar_three[pl.ds(q_me, 1)] = final[None]
        if COMM:
            for d in range(1, 16):
                pltpu.make_async_remote_copy(
                    src_ref=ar_three.at[q_me], dst_ref=ar_three.at[q_me],
                    send_sem=ar_send.at[2], recv_sem=ar_recv.at[2],
                    device_id=group_one(lax.rem(q_me + d, 16)), device_id_type=MESH,
                ).start()

    def finish():
        if COMM:
            batch(ar_three, 15, 2).wait_recv()
        for q in range(16):
            chunk = ar_three[q].astype(F32)
            grad_wvalue[8 * q : 8 * q + 8, :] = chunk[0:8]
            grad_wout[8 * q : 8 * q + 8, :] = chunk[8:16]
            grad_gain[q : q + 1, :] = chunk[16:17]
            if q < K:
                grad_wradial[q : q + 1, :] = chunk[24:25]

    for c in range(2):
        for k in range(K):
            lhs[c, k, :, :N] = (grad_agg[c] * wk[k : k + 1]).astype(BF16)
        pacc[c] = jnp.zeros((3, N, N), F32)

    def pulls(c, role):
        span = slice(c * N, (c + 3) * N)
        both = jnp.concatenate([hc[role, span, :], hg[role, span, :]], axis=1)
        sbuf[...] = dot(lhs[c].reshape(K * N, 2 * N), both, ((1,), (1,))).reshape(K, N, 3 * N)
        near_rows = near(c, role)

        @pl.loop(0, N // ROWS)
        def _(i):
            i0 = pl.multiple_of(i * ROWS, ROWS)
            deltas = deltas_of(c, near_rows, i0)
            ratio = geo[c, role, 0, pl.ds(i0, ROWS), :]
            total = sbuf[K - 1, pl.ds(i0, ROWS), :]
            slope = total
            for k in range(K - 2, -1, -1):
                total = total * ratio + sbuf[k, pl.ds(i0, ROWS), :]
                if k > 0:
                    slope = slope * ratio + total
            slope = slope * ratio
            pull = geo[c, role, 1, pl.ds(i0, ROWS), :] * total - geo[c, role, 2, pl.ds(i0, ROWS), :] * slope
            for n in range(3):
                part = pull * deltas[n]
                pacc[c, n, pl.ds(i0, ROWS), :] += part[:, :N] + part[:, N : 2 * N] + part[:, 2 * N :]

    for c in range(2):
        out_feat[0, c] = (hf[0, own_rows(c), :].astype(F32) + pre[c] * sigs[c]).astype(BF16)
    middle()
    arrive(GRAD, (0, 0), (0, 3))
    for c in range(2):
        gather(c, 0, hg, True)
    for c in range(2):
        pulls(c, 0)
    for col in (1, 2):
        arrive(GRAD, (1, col))
        send(GRAD, RELAY[col])
    arrive(GRAD, (1, 0), (1, 3))
    for c in range(2):
        gather(c, 1, hg, False)
    collect()
    for c in range(2):
        pulls(c, 1)
    arrive(GRAD, (2, 0), (2, 1), (2, 2), (2, 3))
    for c in range(2):
        gather(c, 2, hg, False)
    for c in range(2):
        pulls(c, 2)

    for c in range(2):
        total = usum[c, 0] * wk[0:1]
        for k in range(1, K):
            total = total + usum[c, k] * wk[k : k + 1]
        back = (total * gain[0, own_rows(c), :]).astype(BF16)
        change = dot(back, w_value[...], ((1,), (1,)))
        grad_feat[0, c] = (cot[0, c].astype(F32) + change).astype(BF16)
        for n in range(3):
            scale = 2.0 * (HZ if n == 2 else 1.0)
            grad_pos[0, n, c : c + 1, :] = jnp.sum(pacc[c, n].T, axis=0, keepdims=True) * scale
    finish()
    if COMM:
        for who, copy in sent:
            where_sent(who, copy.wait_send)
        batch(ar_one, 15, 0).wait_send()
        batch(ar_two, 7, 1).wait_send()
        batch(ar_three, 15, 2).wait_send()


def store(*refs):
    count = len(refs) // 2
    sems = refs[-1]
    copies = [pltpu.make_async_copy(refs[n], refs[count + n], sems.at[n]) for n in range(count)]
    for copy in copies:
        copy.start()
    for copy in copies:
        copy.wait()


def on_device(features, positions, bead_types, cell_counts, w_value, w_radial, type_gain, w_out, cotangent):
    vmem = pl.BlockSpec(memory_space=pltpu.VMEM)
    anywhere = pl.BlockSpec(memory_space=pl.ANY)
    shape = jax.ShapeDtypeStruct
    shapes = (
        shape((1, 2, N, N), BF16),
        shape((1, 2, N, N), BF16),
        shape((1, 3, 2, N), F32),
        shape((N, N), F32),
        shape((K, N), F32),
        shape((16, N), F32),
        shape((N, N), F32),
    )
    results = pl.pallas_call(
        kernel,
        out_shape=shapes,
        in_specs=[pl.BlockSpec(memory_space=pltpu.HBM)] * 9,
        out_specs=(vmem,) * 7,
        scratch_shapes=[
            pltpu.VMEM((3, 8, 4 * N), F32),
            pltpu.VMEM((3, 4 * N, N), BF16),
            pltpu.VMEM((3, 4 * N, N), BF16),
            pltpu.VMEM((3, 4 * N, N), BF16),
            pltpu.VMEM((2, 3, N, N), F32),
            pltpu.VMEM((2, 3, K, N, 3 * N), BF16),
            pltpu.VMEM((2, 3, 3, N, 3 * N), F32),
            pltpu.VMEM((2, K, N, N), F32),
            pltpu.VMEM((K, N, 3 * N), F32),
            pltpu.VMEM((2, K, N, 2 * N), BF16),
            pltpu.VMEM((2, 3, N, N), F32),
            pltpu.VMEM((3, 4 * N, N), F32),
            pltpu.VMEM((3, 4 * N, N), F32),
            pltpu.VMEM((3, 16, 4 * N), F32),
            pltpu.VMEM((K, N, N), F32),
            pltpu.VMEM((2, N, K * N), BF16),
            pltpu.VMEM((3, N, 4 * N), F32),
            pltpu.VMEM((1, 3, 2, N), F32),
            pltpu.VMEM((1, 2, N), jnp.int32),
            pltpu.VMEM((1, 2), jnp.int32),
            pltpu.VMEM((N, N), BF16),
            pltpu.VMEM((K, N), F32),
            pltpu.VMEM((16, N), F32),
            pltpu.VMEM((N, N), BF16),
            pltpu.VMEM((1, 2, N, N), BF16),
            pltpu.VMEM((16, 32, N), BF16),
            pltpu.VMEM((16, 32, N), BF16),
            pltpu.VMEM((32, N), BF16),
            pltpu.VMEM((8, 32, N), BF16),
            pltpu.VMEM((16, 32, N), BF16),
            pltpu.SemaphoreType.DMA((10,)),
            pltpu.SemaphoreType.DMA((42,)),
            pltpu.SemaphoreType.DMA((3, 12)),
            pltpu.SemaphoreType.DMA((3,)),
            pltpu.SemaphoreType.DMA((3,)),
        ],
        compiler_params=pltpu.CompilerParams(
            collective_id=0, has_side_effects=True, vmem_limit_bytes=40 * 1024 * 1024
        ),
        cost_estimate=pl.CostEstimate(flops=4_000_000_000, bytes_accessed=1_000_000, transcendentals=4_000_000),
    )(*(pltpu.with_memory_space_constraint(array, pltpu.HBM) for array in (
        features, positions.transpose(0, 2, 1, 3), bead_types, cell_counts,
        w_value, w_radial, type_gain, w_out, cotangent,
    )))
    out = pl.pallas_call(
        store,
        out_shape=shapes,
        in_specs=[anywhere] * 7,
        out_specs=(pl.BlockSpec(memory_space=pltpu.HBM),) * 7,
        scratch_shapes=[pltpu.SemaphoreType.DMA((7,))],
        compiler_params=pltpu.CompilerParams(vmem_limit_bytes=2 * 1024 * 1024),
    )(*results)
    return (out[0], out[1], out[2].transpose(0, 2, 1, 3)) + tuple(out[3:])


def solution(mesh):
    cells = P(("frame", "gx"), "gy", None, None)
    return jax.shard_map(
        on_device,
        mesh=mesh,
        in_specs=(cells, cells, P(("frame", "gx"), "gy", None), P(("frame", "gx"), "gy"), P(), P(), P(), P(), cells),
        out_specs=(cells, cells, cells) + (P("frame", None),) * 4,
        check_vma=False,
    )
```

```python
import jax
import jax.numpy as jnp
from jax import lax
from jax.experimental import pallas as pl
from jax.experimental.pallas import tpu as pltpu
from jax.sharding import PartitionSpec as P

MESH = pl.DeviceIdType.MESH
F32 = jnp.float32
BF16 = jnp.bfloat16
EXACT = lax.Precision.HIGHEST
HZ = 6.0
SOFTEN = 0.01
N = 128
K = 8
NX = 8
NY = 16
GAMMA = 24.5
FAR = 1000.0
POS, VAL, GRAD = 0, 1, 2
ROWS = 16
COMM = True

FIRST = (
    ((0, 1), (1, 1), "O", "all"),
    ((0, 2), (1, 2), "O", "all"),
    ((0, 1), (0, 3), "W", "all"),
    ((0, 2), (0, 0), "E", "all"),
    ((0, 1), (1, 3), "OW", "first"),
    ((0, 1), (2, 3), "RW", "first"),
    ((0, 2), (1, 0), "OE", "last"),
    ((0, 2), (2, 0), "RE", "last"),
)
RELAY = {
    1: (((1, 1), (2, 1), "P", "all"), ((1, 1), (1, 3), "W", "not first"), ((1, 1), (2, 3), "PW", "not first")),
    2: (((1, 2), (2, 2), "P", "all"), ((1, 2), (1, 0), "E", "not last"), ((1, 2), (2, 0), "PE", "not last")),
}


EARLY = ((1, 3), (0, 2))
LATE = ((0, 1), (2, 3))
ALL = ((0, 3), (0, 3))


def dot(a, b, dims=((1,), (0,)), precision=None):
    return lax.dot_general(a, b, (dims, ((), ())), precision=precision, preferred_element_type=F32)


def kernel(
    feat_in, pos_in, types_in, counts_in, w_value_in, w_radial_in, type_gain_in, w_out_in, cot_in,
    out_feat, grad_feat, grad_pos, grad_wvalue, grad_wradial, grad_gain, grad_wout,
    hp, hf, hc, hg, own, ebuf, geo, usum, sbuf, lhs, pacc, proj, gain, onehot, wkt, sct, vt,
    pos, types, counts, w_value, w_radial, type_gain, w_out, cot,
    ar_src, ar_one, ar_mid, ar_two, ar_three, ex_one, ex_mid, ex_two, ex_three,
    load_sem, send_sem, recv_sem, ar_send, ar_recv,
):
    gx = lax.axis_index("gx")
    gy = lax.axis_index("gy")
    zh = lax.rem(gx, 2)
    yy = gx // 2
    side = 1 - 2 * zh
    side_f = side.astype(F32)
    west, east = lax.rem(gy + NY - 1, NY), lax.rem(gy + 1, NY)
    across = lax.rem(gx + side + NX, NX)
    other = lax.rem(gx - side + NX, NX)
    beyond = lax.rem(gx + 2 * side + NX, NX)
    behind = lax.rem(gx - 2 * side + NX, NX)
    dev = {
        "O": (across, gy), "OW": (across, west), "OE": (across, east),
        "RW": (other, west), "RE": (other, east),
        "W": (gx, west), "E": (gx, east),
        "P": (beyond, gy), "PW": (beyond, west), "PE": (beyond, east),
        "QW": (behind, west), "QE": (behind, east),
    }
    dev = {name: {"gx": x, "gy": y} for name, (x, y) in dev.items()}
    quad = gy // 4
    q_me = yy * 4 + lax.rem(gy, 4)
    p_me = zh * 4 + quad

    def group_one(q):
        return {"gx": 2 * (q // 4) + zh, "gy": quad * 4 + lax.rem(q, 4)}

    def group_two(p):
        return {"gx": 2 * yy + p // 4, "gy": lax.rem(p, 4) * 4 + lax.rem(gy, 4)}

    loads = [
        pltpu.make_async_copy(src, dst, load_sem.at[n])
        for n, (src, dst) in enumerate((
            (pos_in, pos), (types_in, types), (counts_in, counts), (w_radial_in, w_radial),
            (feat_in.at[0, 0], hf.at[0, N : 2 * N, :]), (feat_in.at[0, 1], hf.at[0, 2 * N : 3 * N, :]),
            (type_gain_in, type_gain), (w_value_in, w_value), (w_out_in, w_out), (cot_in, cot),
        ))
    ]
    for load in loads[:3]:
        load.start()
    barrier = pltpu.get_barrier_semaphore()
    if COMM:
        for name in ("W", "E", "PW", "PE", "QW", "QE"):
            pl.semaphore_signal(barrier, inc=1, device_id=dev[name], device_id_type=MESH)
        for edge, names in ((0, ("OW", "RW")), (NY - 1, ("OE", "RE"))):
            @pl.when(gy == edge)
            def _():
                for name in names:
                    pl.semaphore_signal(barrier, inc=1, device_id=dev[name], device_id_type=MESH)
        for d in range(1, 16):
            pl.semaphore_signal(barrier, inc=1, device_id=group_one(lax.rem(q_me + d, 16)), device_id_type=MESH)
        for d in range(1, 8):
            pl.semaphore_signal(barrier, inc=1, device_id=group_two(lax.rem(p_me + d, 8)), device_id_type=MESH)
    for load in loads[3:]:
        load.start()

    for load in loads[:3]:
        load.wait()
    lane = lax.broadcasted_iota(jnp.int32, (1, N), 1)
    near_z = []
    for c in range(2):
        missing = jnp.where(lane < counts[:, c : c + 1], 0.0, FAR)
        x, y, z = (pos[0, n, c : c + 1, :] for n in range(3))
        z = z * HZ
        kind = types[0, c : c + 1, :].astype(F32)
        near_z.append(z - missing)
        hp[0, :, (1 + c) * N : (2 + c) * N] = jnp.concatenate(
            [x, y, z + missing, kind, jnp.zeros((4, N), F32)], axis=0
        )

    def slot(kind, place, source=False):
        role, column = place
        if kind == VAL and role == 0 and column in (1, 2) and source:
            return feat_in.at[0, column - 1]
        if kind == POS:
            return hp.at[role, :, column * N : (column + 1) * N]
        return (hf if kind == VAL else hg).at[role, column * N : (column + 1) * N, :]

    sent = []

    def where_sent(who, act):
        if who == "all":
            act()
        else:
            pl.when({
                "first": gy == 0, "not first": gy != 0, "last": gy == NY - 1, "not last": gy != NY - 1
            }[who])(act)

    def send(kind, messages):
        if not COMM:
            return
        for src, dst, to, who in messages:
            copy = pltpu.make_async_remote_copy(
                src_ref=slot(kind, src, True),
                dst_ref=slot(kind, dst),
                send_sem=send_sem.at[len(sent)],
                recv_sem=recv_sem.at[kind, dst[0] * 4 + dst[1]],
                device_id=dev[to],
                device_id_type=MESH,
            )
            where_sent(who, copy.start)
            sent.append((who, copy))

    def arrive(kind, *places):
        if not COMM:
            return
        for place in places:
            pltpu.make_async_remote_copy(
                src_ref=slot(kind, place),
                dst_ref=slot(kind, place),
                send_sem=send_sem.at[0],
                recv_sem=recv_sem.at[kind, place[0] * 4 + place[1]],
                device_id=dev["O"],
                device_id_type=MESH,
            ).wait_recv()

    if COMM:
        at_edge = lax.rem(gy + 1, NY) < 2

        @pl.when(at_edge)
        def _():
            pl.semaphore_wait(barrier, 6 + 15 + 7 + 2)

        @pl.when(jnp.logical_not(at_edge))
        def _():
            pl.semaphore_wait(barrier, 6 + 15 + 7)
    send(POS, FIRST)
    send(VAL, FIRST)

    for load in loads[3:]:
        load.wait()
    for c in range(2):
        for n, row in enumerate((pos[0, 0, c : c + 1, :], pos[0, 1, c : c + 1, :], near_z[c])):
            own[c, n] = jnp.broadcast_to(row, (N, N)).T
    basis = lax.broadcasted_iota(jnp.int32, (K, N), 0).astype(F32)
    fold = jnp.exp(-0.5 * basis * basis)
    wk = w_radial[...] * fold
    for k in range(K):
        wkt[k] = jnp.broadcast_to(wk[k : k + 1], (N, N)).T

    window = lax.broadcasted_iota(jnp.int32, (1, 3 * N), 1)
    shift_y = (window // N - 1).astype(F32)

    def near(c, role):
        block = hp[role, :, c * N : (c + 3) * N]
        shift_x = (0.0, side_f, -side_f)[role]
        return block[0:1] + shift_x, block[1:2] + shift_y, block[2:3]

    def deltas_of(c, near_rows, i0):
        deltas = []
        for n in range(3):
            mine = own[c, n, pl.ds(i0, ROWS), :]
            deltas.append(near_rows[n] - jnp.concatenate([mine] * 3, axis=1))
        return deltas

    def weights(c, role):
        near_rows = near(c, role)

        @pl.loop(0, N // ROWS)
        def _(i):
            i0 = pl.multiple_of(i * ROWS, ROWS)
            dx, dy, dz = deltas_of(c, near_rows, i0)
            dist = dx * dx + dy * dy + dz * dz
            if role == 0:
                row = lax.broadcasted_iota(jnp.int32, (ROWS, 3 * N), 0) + (i0 + N)
                col = lax.broadcasted_iota(jnp.int32, (ROWS, 3 * N), 1)
                dist = jnp.where(row == col, 2.0, dist)
            inside = jnp.maximum(1.0 - dist, 0.0)
            soft = (1.0 + SOFTEN) - inside
            inverse = lax.rsqrt(soft)
            ratio = jnp.exp((K - 1.0) * (soft * inverse))
            lead = inside * jnp.exp(-GAMMA * soft)
            value = inside * lead
            geo[c, role, 0, pl.ds(i0, ROWS), :] = ratio
            geo[c, role, 1, pl.ds(i0, ROWS), :] = 2.0 * lead + GAMMA * value
            geo[c, role, 2, pl.ds(i0, ROWS), :] = value * inverse * (GAMMA / (K - 1.0))
            for k in range(K):
                ebuf[c, role, k, pl.ds(i0, ROWS), :] = value.astype(BF16)
                if k < K - 1:
                    value = value * ratio

    def gather(c, role, table, first, part=ALL):
        low, high = part[c]
        got = dot(
            ebuf[c, role, :, :, low * N : high * N].reshape(K * N, (high - low) * N),
            table[role, (c + low) * N : (c + high) * N, :],
        ).reshape(K, N, N)
        if first:
            usum[c] = got
        else:
            usum[c] += got

    kind_of = lax.broadcasted_iota(jnp.int32, (16, 4 * N), 0).astype(F32)

    def gains(role):
        hot = jnp.where(kind_of == hp[role, 3:4, :], 1.0, 0.0)
        onehot[role] = hot
        gain[role] = dot(hot, type_gain[...], ((0,), (0,)), EXACT)

    def values(role, low=0, high=4):
        span = slice(low * N, high * N)
        projected = dot(hf[role, span, :], w_value[...])
        proj[role, span, :] = projected
        hc[role, span, :] = (projected * gain[role, span, :]).astype(BF16)

    arrive(POS, (0, 0), (0, 3))
    for c in range(2):
        weights(c, 0)
    gains(0)
    for col in (1, 2):
        arrive(POS, (1, col))
        send(POS, RELAY[col])
    arrive(VAL, (0, 0), (0, 3))
    values(0)
    for c in range(2):
        gather(c, 0, hc, True)
    for col in (1, 2):
        arrive(VAL, (1, col))
        send(VAL, RELAY[col])
    for c in range(2):
        value = hc[0, (1 + c) * N : (2 + c) * N, :].astype(F32)
        for k in range(K):
            lhs[c, k, :, N:] = (value * wk[k : k + 1]).astype(BF16)
    arrive(POS, (1, 0), (1, 3))
    for c in range(2):
        weights(c, 1)
    gains(1)
    arrive(POS, (2, 0), (2, 1), (2, 2), (2, 3))
    for c in range(2):
        weights(c, 2)
    gains(2)
    values(1, 1, 3)
    for c in range(2):
        gather(c, 1, hc, False, EARLY)
    arrive(VAL, (1, 0), (1, 3))
    values(1, 0, 1)
    values(1, 3, 4)
    for c in range(2):
        gather(c, 1, hc, False, LATE)
    arrive(VAL, (2, 0), (2, 1), (2, 2), (2, 3))
    values(2)

    def own_rows(c):
        return slice((1 + c) * N, (2 + c) * N)

    pre = []
    halves = []
    grad_pre = []
    sigs = []
    grad_agg = []
    for c in range(2):
        gather(c, 2, hc, False)
        total = usum[c, 0] * wk[0:1]
        for k in range(1, K):
            total = total + usum[c, k] * wk[k : k + 1]
        halves.append(total.astype(BF16))
        pre.append(dot(halves[c], w_out[...]))
        sig = jax.nn.sigmoid(pre[c])
        sigs.append(sig)
        grad_pre.append((cot[0, c].astype(F32) * sig * (1.0 + pre[c] * (1.0 - sig))).astype(BF16))
        half = dot(grad_pre[c], w_out[...], ((1,), (1,))).astype(BF16)
        hg[0, own_rows(c), :] = half
        grad_agg.append(half.astype(F32))
        send(GRAD, [message for message in FIRST if message[0] == (0, 1 + c)])

    for c in range(2):
        flipped = grad_agg[c].T
        for k in range(K):
            sct[c, :, k * N : (k + 1) * N] = (flipped * wkt[k]).astype(BF16)
    for role in range(3):
        vt[role, :, 3 * N :] = jnp.zeros((N, N), F32)
        vt[role, :, : 3 * N] = dot(sct[0], ebuf[0, role].reshape(K * N, 3 * N))
        vt[role, :, N:] += dot(sct[1], ebuf[1, role].reshape(K * N, 3 * N))
    value_part = jnp.zeros((N, N), F32)
    gain_part = jnp.zeros((16, N), F32)
    for role in range(3):
        given = vt[role].T
        half = (given * gain[role]).astype(BF16)
        value_part = value_part + dot(hf[role], half, ((0,), (0,)))
        gain_part = gain_part + dot(onehot[role], given * proj[role], precision=EXACT)
    wout_part = dot(halves[0], grad_pre[0], ((0,), (0,))) + dot(halves[1], grad_pre[1], ((0,), (0,)))
    rows = []
    for k in range(K):
        rows.append(jnp.sum(grad_agg[0] * usum[0, k] + grad_agg[1] * usum[1, k], axis=0, keepdims=True))
    wradial_part = jnp.concatenate(rows, axis=0) * fold

    for q in range(16):
        own_q = slice(8 * q, 8 * q + 8)
        ar_src[q] = jnp.concatenate([value_part[own_q], wout_part[own_q]], axis=0).astype(BF16)
    ar_src[16] = gain_part.astype(BF16)
    ar_src[17] = jnp.concatenate([wradial_part, wradial_part], axis=0).astype(BF16)
    ar_one[pl.ds(q_me, 1)] = ar_src[pl.ds(q_me, 1)]

    def batch(buffer, count, phase):
        return pltpu.make_async_remote_copy(
            src_ref=buffer.at[pl.ds(0, count)], dst_ref=buffer.at[pl.ds(0, count)],
            send_sem=ar_send.at[phase], recv_sem=ar_recv.at[phase],
            device_id=dev["O"], device_id_type=MESH,
        )

    if COMM:
        for d in range(1, 16):
            q = lax.rem(q_me + d, 16)
            pltpu.make_async_remote_copy(
                src_ref=ar_src.at[q], dst_ref=ar_one.at[q_me],
                send_sem=ar_send.at[0], recv_sem=ar_recv.at[0],
                device_id=group_one(q), device_id_type=MESH,
            ).start()

    def extra(j):
        return pltpu.make_async_remote_copy(
            src_ref=ar_src.at[16 + j], dst_ref=ex_one.at[q_me],
            send_sem=ar_send.at[3 + j], recv_sem=ar_recv.at[3],
            device_id=group_one(j), device_id_type=MESH,
        )

    def extra_final(j):
        return pltpu.make_async_remote_copy(
            src_ref=ex_three.at[j], dst_ref=ex_three.at[j],
            send_sem=ar_send.at[6], recv_sem=ar_recv.at[5 + j],
            device_id=dev["W"], device_id_type=MESH,
        )

    for j in range(2):
        @pl.when(q_me == j)
        def _():
            ex_one[pl.ds(j, 1)] = ar_src[pl.ds(16 + j, 1)]

        if COMM:
            pl.when(q_me != j)(extra(j).start)

    def middle():
        if COMM:
            batch(ar_one, 15, 0).wait_recv()
        ar_mid[...] = jnp.sum(ar_one[...].astype(F32), axis=0).astype(BF16)
        ar_two[pl.ds(p_me, 1)] = ar_mid[...][None]
        if COMM:
            for d in range(1, 8):
                pltpu.make_async_remote_copy(
                    src_ref=ar_mid, dst_ref=ar_two.at[p_me],
                    send_sem=ar_send.at[1], recv_sem=ar_recv.at[1],
                    device_id=group_two(lax.rem(p_me + d, 8)), device_id_type=MESH,
                ).start()

            @pl.when(q_me < 2)
            def _():
                batch(ex_one, 15, 3).wait_recv()
                ex_mid[...] = jnp.sum(ex_one[...].astype(F32), axis=0).astype(BF16)
                ex_two[pl.ds(p_me, 1)] = ex_mid[...][None]
                for d in range(1, 8):
                    pltpu.make_async_remote_copy(
                        src_ref=ex_mid, dst_ref=ex_two.at[p_me],
                        send_sem=ar_send.at[5], recv_sem=ar_recv.at[4],
                        device_id=group_two(lax.rem(p_me + d, 8)), device_id_type=MESH,
                    ).start()

    def collect():
        if COMM:
            batch(ar_two, 7, 1).wait_recv()
        final = jnp.sum(ar_two[...].astype(F32), axis=0).astype(BF16)
        ar_three[pl.ds(q_me, 1)] = final[None]
        if COMM:
            for d in range(1, 16):
                pltpu.make_async_remote_copy(
                    src_ref=ar_three.at[q_me], dst_ref=ar_three.at[q_me],
                    send_sem=ar_send.at[2], recv_sem=ar_recv.at[2],
                    device_id=group_one(lax.rem(q_me + d, 16)), device_id_type=MESH,
                ).start()

            for j in range(2):
                @pl.when(q_me == j)
                def _():
                    batch(ex_two, 7, 4).wait_recv()
                    ex_three[j] = jnp.sum(ex_two[...].astype(F32), axis=0).astype(BF16)
                    for d in range(1, 16):
                        pltpu.make_async_remote_copy(
                            src_ref=ex_three.at[j], dst_ref=ex_three.at[j],
                            send_sem=ar_send.at[6], recv_sem=ar_recv.at[5 + j],
                            device_id=group_one((j + d) % 16), device_id_type=MESH,
                        ).start()

    def finish():
        if COMM:
            batch(ar_three, 15, 2).wait_recv()
            for j in range(2):
                pl.when(q_me != j)(extra_final(j).wait_recv)
        for q in range(16):
            chunk = ar_three[q].astype(F32)
            grad_wvalue[8 * q : 8 * q + 8, :] = chunk[0:8]
            grad_wout[8 * q : 8 * q + 8, :] = chunk[8:16]
        grad_gain[...] = ex_three[0].astype(F32)
        grad_wradial[...] = ex_three[1].astype(F32)[:K]

    for c in range(2):
        for k in range(K):
            lhs[c, k, :, :N] = (grad_agg[c] * wk[k : k + 1]).astype(BF16)
        pacc[c] = jnp.zeros((3, N, N), F32)

    def pulls(c, role, part=ALL):
        low, high = part[c]
        wide = high - low
        rows = 64 // wide if wide < 3 else ROWS
        span = slice((c + low) * N, (c + high) * N)
        lanes = slice(low * N, high * N)
        both = jnp.concatenate([hc[role, span, :], hg[role, span, :]], axis=1)
        sbuf[:, :, : wide * N] = dot(lhs[c].reshape(K * N, 2 * N), both, ((1,), (1,))).reshape(K, N, wide * N)
        near_rows = [row[:, lanes] for row in near(c, role)]

        @pl.loop(0, N // rows)
        def _(i):
            some = pl.ds(pl.multiple_of(i * rows, rows), rows)
            ratio = geo[c, role, 0, some, lanes]
            total = sbuf[K - 1, some, : wide * N]
            slope = total
            for k in range(K - 2, -1, -1):
                total = total * ratio + sbuf[k, some, : wide * N]
                if k > 0:
                    slope = slope * ratio + total
            slope = slope * ratio
            pull = geo[c, role, 1, some, lanes] * total - geo[c, role, 2, some, lanes] * slope
            for n in range(3):
                mine = own[c, n, some, :]
                moved = pacc[c, n, some, :]
                for w in range(wide):
                    block = slice(w * N, (w + 1) * N)
                    moved = moved + pull[:, block] * (near_rows[n][:, block] - mine)
                pacc[c, n, some, :] = moved

    for c in range(2):
        out_feat[0, c] = (hf[0, own_rows(c), :].astype(F32) + pre[c] * sigs[c]).astype(BF16)
    for c in range(2):
        gather(c, 0, hg, True, EARLY)
    for c in range(2):
        pulls(c, 0, EARLY)
    middle()
    arrive(GRAD, (0, 0), (0, 3))
    for c in range(2):
        gather(c, 0, hg, False, LATE)
    for c in range(2):
        pulls(c, 0, LATE)
    for col in (1, 2):
        arrive(GRAD, (1, col))
        send(GRAD, RELAY[col])
    for c in range(2):
        gather(c, 1, hg, False, EARLY)
    for c in range(2):
        pulls(c, 1, EARLY)
    collect()
    arrive(GRAD, (1, 0), (1, 3))
    for c in range(2):
        gather(c, 1, hg, False, LATE)
    for c in range(2):
        pulls(c, 1, LATE)
    arrive(GRAD, (2, 0), (2, 1), (2, 2), (2, 3))
    for c in range(2):
        gather(c, 2, hg, False)
    for c in range(2):
        pulls(c, 2)

    for c in range(2):
        total = usum[c, 0] * wk[0:1]
        for k in range(1, K):
            total = total + usum[c, k] * wk[k : k + 1]
        back = (total * gain[0, own_rows(c), :]).astype(BF16)
        change = dot(back, w_value[...], ((1,), (1,)))
        grad_feat[0, c] = (cot[0, c].astype(F32) + change).astype(BF16)
        for n in range(3):
            scale = 2.0 * (HZ if n == 2 else 1.0)
            grad_pos[0, n, c : c + 1, :] = jnp.sum(pacc[c, n].T, axis=0, keepdims=True) * scale
    finish()
    if COMM:
        for who, copy in sent:
            where_sent(who, copy.wait_send)
        batch(ar_one, 15, 0).wait_send()
        batch(ar_two, 7, 1).wait_send()
        batch(ar_three, 15, 2).wait_send()
        for j in range(2):
            pl.when(q_me != j)(extra(j).wait_send)

        @pl.when(q_me < 2)
        def _():
            pltpu.make_async_remote_copy(
                src_ref=ex_two.at[pl.ds(0, 7)], dst_ref=ex_two.at[pl.ds(0, 7)],
                send_sem=ar_send.at[5], recv_sem=ar_recv.at[4], device_id=dev["W"], device_id_type=MESH,
            ).wait_send()
            pltpu.make_async_remote_copy(
                src_ref=ex_one.at[pl.ds(0, 15)], dst_ref=ex_one.at[pl.ds(0, 15)],
                send_sem=ar_send.at[6], recv_sem=ar_recv.at[3], device_id=dev["W"], device_id_type=MESH,
            ).wait_send()


def store(*refs):
    count = len(refs) // 2
    sems = refs[-1]
    copies = [pltpu.make_async_copy(refs[n], refs[count + n], sems.at[n]) for n in range(count)]
    for copy in copies:
        copy.start()
    for copy in copies:
        copy.wait()


def on_device(features, positions, bead_types, cell_counts, w_value, w_radial, type_gain, w_out, cotangent):
    vmem = pl.BlockSpec(memory_space=pltpu.VMEM)
    anywhere = pl.BlockSpec(memory_space=pl.ANY)
    shape = jax.ShapeDtypeStruct
    shapes = (
        shape((1, 2, N, N), BF16),
        shape((1, 2, N, N), BF16),
        shape((1, 3, 2, N), F32),
        shape((N, N), F32),
        shape((K, N), F32),
        shape((16, N), F32),
        shape((N, N), F32),
    )
    results = pl.pallas_call(
        kernel,
        out_shape=shapes,
        in_specs=[pl.BlockSpec(memory_space=pltpu.HBM)] * 9,
        out_specs=(vmem,) * 7,
        scratch_shapes=[
            pltpu.VMEM((3, 8, 4 * N), F32),
            pltpu.VMEM((3, 4 * N, N), BF16),
            pltpu.VMEM((3, 4 * N, N), BF16),
            pltpu.VMEM((3, 4 * N, N), BF16),
            pltpu.VMEM((2, 3, N, N), F32),
            pltpu.VMEM((2, 3, K, N, 3 * N), BF16),
            pltpu.VMEM((2, 3, 3, N, 3 * N), F32),
            pltpu.VMEM((2, K, N, N), F32),
            pltpu.VMEM((K, N, 3 * N), F32),
            pltpu.VMEM((2, K, N, 2 * N), BF16),
            pltpu.VMEM((2, 3, N, N), F32),
            pltpu.VMEM((3, 4 * N, N), F32),
            pltpu.VMEM((3, 4 * N, N), F32),
            pltpu.VMEM((3, 16, 4 * N), F32),
            pltpu.VMEM((K, N, N), F32),
            pltpu.VMEM((2, N, K * N), BF16),
            pltpu.VMEM((3, N, 4 * N), F32),
            pltpu.VMEM((1, 3, 2, N), F32),
            pltpu.VMEM((1, 2, N), jnp.int32),
            pltpu.VMEM((1, 2), jnp.int32),
            pltpu.VMEM((N, N), BF16),
            pltpu.VMEM((K, N), F32),
            pltpu.VMEM((16, N), F32),
            pltpu.VMEM((N, N), BF16),
            pltpu.VMEM((1, 2, N, N), BF16),
            pltpu.VMEM((18, 16, N), BF16),
            pltpu.VMEM((16, 16, N), BF16),
            pltpu.VMEM((16, N), BF16),
            pltpu.VMEM((8, 16, N), BF16),
            pltpu.VMEM((16, 16, N), BF16),
            pltpu.VMEM((16, 16, N), BF16),
            pltpu.VMEM((16, N), BF16),
            pltpu.VMEM((8, 16, N), BF16),
            pltpu.VMEM((2, 16, N), BF16),
            pltpu.SemaphoreType.DMA((10,)),
            pltpu.SemaphoreType.DMA((42,)),
            pltpu.SemaphoreType.DMA((3, 12)),
            pltpu.SemaphoreType.DMA((7,)),
            pltpu.SemaphoreType.DMA((7,)),
        ],
        compiler_params=pltpu.CompilerParams(
            collective_id=0, has_side_effects=True, vmem_limit_bytes=40 * 1024 * 1024
        ),
        cost_estimate=pl.CostEstimate(flops=4_000_000_000, bytes_accessed=1_000_000, transcendentals=4_000_000),
    )(*(pltpu.with_memory_space_constraint(array, pltpu.HBM) for array in (
        features, positions.transpose(0, 2, 1, 3), bead_types, cell_counts,
        w_value, w_radial, type_gain, w_out, cotangent,
    )))
    out = pl.pallas_call(
        store,
        out_shape=shapes,
        in_specs=[anywhere] * 7,
        out_specs=(pl.BlockSpec(memory_space=pltpu.HBM),) * 7,
        scratch_shapes=[pltpu.SemaphoreType.DMA((7,))],
        compiler_params=pltpu.CompilerParams(vmem_limit_bytes=2 * 1024 * 1024),
    )(*results)
    return (out[0], out[1], out[2].transpose(0, 2, 1, 3)) + tuple(out[3:])


def solution(mesh):
    cells = P(("frame", "gx"), "gy", None, None)
    return jax.shard_map(
        on_device,
        mesh=mesh,
        in_specs=(cells, cells, P(("frame", "gx"), "gy", None), P(("frame", "gx"), "gy"), P(), P(), P(), P(), cells),
        out_specs=(cells, cells, cells) + (P("frame", None),) * 4,
        check_vma=False,
    )
```

```python
import jax
import jax.numpy as jnp
from jax import lax
from jax.experimental import pallas as pl
from jax.experimental.pallas import tpu as pltpu
from jax.sharding import PartitionSpec as P

MESH = pl.DeviceIdType.MESH
F32 = jnp.float32
BF16 = jnp.bfloat16
EXACT = lax.Precision.HIGHEST
HZ = 6.0
SOFTEN = 0.01
N = 128
K = 8
NX = 8
NY = 16
GAMMA = 24.5
FAR = 1000.0
POS, VAL, GRAD = 0, 1, 2
ROWS = 16
COMM = True

FIRST = (
    ((0, 1), (1, 1), "O", "all"),
    ((0, 2), (1, 2), "O", "all"),
    ((0, 1), (0, 3), "W", "all"),
    ((0, 2), (0, 0), "E", "all"),
    ((0, 1), (1, 3), "OW", "first"),
    ((0, 1), (2, 3), "RW", "first"),
    ((0, 2), (1, 0), "OE", "last"),
    ((0, 2), (2, 0), "RE", "last"),
)
RELAY = {
    1: (((1, 1), (2, 3), "PW", "not first"), ((1, 1), (2, 1), "P", "all"), ((1, 1), (1, 3), "W", "not first")),
    2: (((1, 2), (2, 0), "PE", "not last"), ((1, 2), (2, 2), "P", "all"), ((1, 2), (1, 0), "E", "not last")),
}


EARLY = ((1, 3), (0, 2))
LATE = ((0, 1), (2, 3))
ALL = ((0, 3), (0, 3))


def dot(a, b, dims=((1,), (0,)), precision=None):
    return lax.dot_general(a, b, (dims, ((), ())), precision=precision, preferred_element_type=F32)


def kernel(
    feat_in, pos_in, types_in, counts_in, w_value_in, w_radial_in, type_gain_in, w_out_in, cot_in,
    out_feat, grad_feat, grad_pos, grad_wvalue, grad_wradial, grad_gain, grad_wout,
    hp, hf, hc, hg, own, ebuf, geo, usum, sbuf, lhs, pacc, proj, gain, onehot, wkt, sct, vt,
    pos, types, counts, w_value, w_radial, type_gain, w_out, cot,
    ar_src, ar_one, ar_mid, ar_two, ar_three, ex_one, ex_mid, ex_two, ex_three,
    load_sem, send_sem, recv_sem, ar_send, ar_recv,
):
    gx = lax.axis_index("gx")
    gy = lax.axis_index("gy")
    zh = lax.rem(gx, 2)
    yy = gx // 2
    side = 1 - 2 * zh
    side_f = side.astype(F32)
    west, east = lax.rem(gy + NY - 1, NY), lax.rem(gy + 1, NY)
    across = lax.rem(gx + side + NX, NX)
    other = lax.rem(gx - side + NX, NX)
    beyond = lax.rem(gx + 2 * side + NX, NX)
    behind = lax.rem(gx - 2 * side + NX, NX)
    dev = {
        "O": (across, gy), "OW": (across, west), "OE": (across, east),
        "RW": (other, west), "RE": (other, east),
        "W": (gx, west), "E": (gx, east),
        "P": (beyond, gy), "PW": (beyond, west), "PE": (beyond, east),
        "QW": (behind, west), "QE": (behind, east),
    }
    dev = {name: {"gx": x, "gy": y} for name, (x, y) in dev.items()}
    quad = gy // 4
    q_me = yy * 4 + lax.rem(gy, 4)
    p_me = zh * 4 + quad

    def group_one(q):
        return {"gx": 2 * (q // 4) + zh, "gy": quad * 4 + lax.rem(q, 4)}

    def group_two(p):
        return {"gx": 2 * yy + p // 4, "gy": lax.rem(p, 4) * 4 + lax.rem(gy, 4)}

    loads = [
        pltpu.make_async_copy(src, dst, load_sem.at[n])
        for n, (src, dst) in enumerate((
            (pos_in, pos), (types_in, types), (counts_in, counts), (w_radial_in, w_radial),
            (feat_in.at[0, 0], hf.at[0, N : 2 * N, :]), (feat_in.at[0, 1], hf.at[0, 2 * N : 3 * N, :]),
            (type_gain_in, type_gain), (w_value_in, w_value), (w_out_in, w_out), (cot_in, cot),
        ))
    ]
    for load in loads[:3]:
        load.start()
    barrier = pltpu.get_barrier_semaphore()
    if COMM:
        for name in ("W", "E", "PW", "PE", "QW", "QE"):
            pl.semaphore_signal(barrier, inc=1, device_id=dev[name], device_id_type=MESH)
        for edge, names in ((0, ("OW", "RW")), (NY - 1, ("OE", "RE"))):
            @pl.when(gy == edge)
            def _():
                for name in names:
                    pl.semaphore_signal(barrier, inc=1, device_id=dev[name], device_id_type=MESH)
        for d in range(1, 16):
            pl.semaphore_signal(barrier, inc=1, device_id=group_one(lax.rem(q_me + d, 16)), device_id_type=MESH)
        for d in range(1, 8):
            pl.semaphore_signal(barrier, inc=1, device_id=group_two(lax.rem(p_me + d, 8)), device_id_type=MESH)
    for load in loads[3:]:
        load.start()

    for load in loads[:3]:
        load.wait()
    lane = lax.broadcasted_iota(jnp.int32, (1, N), 1)
    near_z = []
    for c in range(2):
        missing = jnp.where(lane < counts[:, c : c + 1], 0.0, FAR)
        x, y, z = (pos[0, n, c : c + 1, :] for n in range(3))
        z = z * HZ
        kind = types[0, c : c + 1, :].astype(F32)
        near_z.append(z - missing)
        hp[0, :, (1 + c) * N : (2 + c) * N] = jnp.concatenate(
            [x, y, z + missing, kind, jnp.zeros((4, N), F32)], axis=0
        )

    def slot(kind, place, source=False):
        role, column = place
        if kind == VAL and role == 0 and column in (1, 2) and source:
            return feat_in.at[0, column - 1]
        if kind == POS:
            return hp.at[role, :, column * N : (column + 1) * N]
        return (hf if kind == VAL else hg).at[role, column * N : (column + 1) * N, :]

    sent = []

    def where_sent(who, act):
        if who == "all":
            act()
        else:
            pl.when({
                "first": gy == 0, "not first": gy != 0, "last": gy == NY - 1, "not last": gy != NY - 1
            }[who])(act)

    def send(kind, messages):
        if not COMM:
            return
        for src, dst, to, who in messages:
            copy = pltpu.make_async_remote_copy(
                src_ref=slot(kind, src, True),
                dst_ref=slot(kind, dst),
                send_sem=send_sem.at[len(sent)],
                recv_sem=recv_sem.at[kind, dst[0] * 4 + dst[1]],
                device_id=dev[to],
                device_id_type=MESH,
            )
            where_sent(who, copy.start)
            sent.append((who, copy))

    def arrive(kind, *places):
        if not COMM:
            return
        for place in places:
            pltpu.make_async_remote_copy(
                src_ref=slot(kind, place),
                dst_ref=slot(kind, place),
                send_sem=send_sem.at[0],
                recv_sem=recv_sem.at[kind, place[0] * 4 + place[1]],
                device_id=dev["O"],
                device_id_type=MESH,
            ).wait_recv()

    if COMM:
        at_edge = lax.rem(gy + 1, NY) < 2

        @pl.when(at_edge)
        def _():
            pl.semaphore_wait(barrier, 6 + 15 + 7 + 2)

        @pl.when(jnp.logical_not(at_edge))
        def _():
            pl.semaphore_wait(barrier, 6 + 15 + 7)
    send(POS, FIRST)
    send(VAL, FIRST)

    for load in loads[3:]:
        load.wait()
    for c in range(2):
        for n, row in enumerate((pos[0, 0, c : c + 1, :], pos[0, 1, c : c + 1, :], near_z[c])):
            own[c, n] = jnp.broadcast_to(row, (N, N)).T
    basis = lax.broadcasted_iota(jnp.int32, (K, N), 0).astype(F32)
    fold = jnp.exp(-0.5 * basis * basis)
    wk = w_radial[...] * fold
    for k in range(K):
        wkt[k] = jnp.broadcast_to(wk[k : k + 1], (N, N)).T

    window = lax.broadcasted_iota(jnp.int32, (1, 3 * N), 1)
    shift_y = (window // N - 1).astype(F32)

    def near(c, role):
        block = hp[role, :, c * N : (c + 3) * N]
        shift_x = (0.0, side_f, -side_f)[role]
        return block[0:1] + shift_x, block[1:2] + shift_y, block[2:3]

    def deltas_of(c, near_rows, i0):
        deltas = []
        for n in range(3):
            mine = own[c, n, pl.ds(i0, ROWS), :]
            deltas.append(near_rows[n] - jnp.concatenate([mine] * 3, axis=1))
        return deltas

    def weights(c, role):
        near_rows = near(c, role)

        @pl.loop(0, N // ROWS)
        def _(i):
            i0 = pl.multiple_of(i * ROWS, ROWS)
            dx, dy, dz = deltas_of(c, near_rows, i0)
            dist = dx * dx + dy * dy + dz * dz
            if role == 0:
                row = lax.broadcasted_iota(jnp.int32, (ROWS, 3 * N), 0) + (i0 + N)
                col = lax.broadcasted_iota(jnp.int32, (ROWS, 3 * N), 1)
                dist = jnp.where(row == col, 2.0, dist)
            inside = jnp.maximum(1.0 - dist, 0.0)
            soft = (1.0 + SOFTEN) - inside
            inverse = lax.rsqrt(soft)
            ratio = jnp.exp((K - 1.0) * (soft * inverse))
            lead = inside * jnp.exp(-GAMMA * soft)
            value = inside * lead
            geo[c, role, 0, pl.ds(i0, ROWS), :] = ratio
            geo[c, role, 1, pl.ds(i0, ROWS), :] = 2.0 * lead + GAMMA * value
            geo[c, role, 2, pl.ds(i0, ROWS), :] = value * inverse * (GAMMA / (K - 1.0))
            for k in range(K):
                ebuf[c, role, k, pl.ds(i0, ROWS), :] = value.astype(BF16)
                if k < K - 1:
                    value = value * ratio

    def gather(c, role, table, first, part=ALL):
        low, high = part[c]
        got = dot(
            ebuf[c, role, :, :, low * N : high * N].reshape(K * N, (high - low) * N),
            table[role, (c + low) * N : (c + high) * N, :],
        ).reshape(K, N, N)
        if first:
            usum[c] = got
        else:
            usum[c] += got

    kind_of = lax.broadcasted_iota(jnp.int32, (16, 4 * N), 0).astype(F32)

    def gains(role):
        hot = jnp.where(kind_of == hp[role, 3:4, :], 1.0, 0.0)
        onehot[role] = hot
        gain[role] = dot(hot, type_gain[...], ((0,), (0,)), EXACT)

    def values(role, low=0, high=4):
        span = slice(low * N, high * N)
        projected = dot(hf[role, span, :], w_value[...])
        proj[role, span, :] = projected
        hc[role, span, :] = (projected * gain[role, span, :]).astype(BF16)

    arrive(POS, (0, 0), (0, 3))
    for c in range(2):
        weights(c, 0)
    gains(0)
    for col in (1, 2):
        arrive(POS, (1, col))
        send(POS, RELAY[col])
    arrive(VAL, (0, 0), (0, 3))
    values(0)
    for c in range(2):
        gather(c, 0, hc, True)
    for col in (1, 2):
        arrive(VAL, (1, col))
        send(VAL, RELAY[col])
    for c in range(2):
        value = hc[0, (1 + c) * N : (2 + c) * N, :].astype(F32)
        for k in range(K):
            lhs[c, k, :, N:] = (value * wk[k : k + 1]).astype(BF16)
    arrive(POS, (1, 0), (1, 3))
    for c in range(2):
        weights(c, 1)
    gains(1)
    arrive(POS, (2, 0), (2, 1), (2, 2), (2, 3))
    for c in range(2):
        weights(c, 2)
    gains(2)
    values(1, 1, 3)
    for c in range(2):
        gather(c, 1, hc, False, EARLY)
    arrive(VAL, (1, 0), (1, 3))
    values(1, 0, 1)
    values(1, 3, 4)
    for c in range(2):
        gather(c, 1, hc, False, LATE)
    arrive(VAL, (2, 0), (2, 1), (2, 2), (2, 3))
    values(2)

    def own_rows(c):
        return slice((1 + c) * N, (2 + c) * N)

    early_sent = len(sent)
    pre = []
    halves = []
    grad_pre = []
    sigs = []
    grad_agg = []
    for c in range(2):
        gather(c, 2, hc, False)
        total = usum[c, 0] * wk[0:1]
        for k in range(1, K):
            total = total + usum[c, k] * wk[k : k + 1]
        halves.append(total.astype(BF16))
        pre.append(dot(halves[c], w_out[...]))
        sig = jax.nn.sigmoid(pre[c])
        sigs.append(sig)
        grad_pre.append((cot[0, c].astype(F32) * sig * (1.0 + pre[c] * (1.0 - sig))).astype(BF16))
        half = dot(grad_pre[c], w_out[...], ((1,), (1,))).astype(BF16)
        hg[0, own_rows(c), :] = half
        grad_agg.append(half.astype(F32))
        send(GRAD, [message for message in FIRST if message[0] == (0, 1 + c)])

    for c in range(2):
        flipped = grad_agg[c].T
        for k in range(K):
            sct[c, :, k * N : (k + 1) * N] = (flipped * wkt[k]).astype(BF16)
    for role in range(3):
        vt[role, :, 3 * N :] = jnp.zeros((N, N), F32)
        vt[role, :, : 3 * N] = dot(sct[0], ebuf[0, role].reshape(K * N, 3 * N))
        vt[role, :, N:] += dot(sct[1], ebuf[1, role].reshape(K * N, 3 * N))
    value_part = jnp.zeros((N, N), F32)
    gain_part = jnp.zeros((16, N), F32)
    for role in range(3):
        given = vt[role].T
        half = (given * gain[role]).astype(BF16)
        value_part = value_part + dot(hf[role], half, ((0,), (0,)))
        product = given * proj[role]
        upper = product.astype(BF16)
        lower = (product - upper.astype(F32)).astype(BF16)
        both = dot(onehot[role].astype(BF16), jnp.concatenate([upper, lower], axis=1))
        gain_part = gain_part + (both[:, :N] + both[:, N:])
    wout_part = dot(halves[0], grad_pre[0], ((0,), (0,))) + dot(halves[1], grad_pre[1], ((0,), (0,)))
    rows = []
    for k in range(K):
        rows.append(jnp.sum(grad_agg[0] * usum[0, k] + grad_agg[1] * usum[1, k], axis=0, keepdims=True))
    wradial_part = jnp.concatenate(rows, axis=0) * fold

    for q in range(16):
        own_q = slice(8 * q, 8 * q + 8)
        ar_src[q] = jnp.concatenate([value_part[own_q], wout_part[own_q]], axis=0).astype(BF16)
    ar_src[16] = gain_part.astype(BF16)
    ar_src[17] = jnp.concatenate([wradial_part, wradial_part], axis=0).astype(BF16)
    ar_one[pl.ds(q_me, 1)] = ar_src[pl.ds(q_me, 1)]

    def batch(buffer, count, phase):
        return pltpu.make_async_remote_copy(
            src_ref=buffer.at[pl.ds(0, count)], dst_ref=buffer.at[pl.ds(0, count)],
            send_sem=ar_send.at[phase], recv_sem=ar_recv.at[phase],
            device_id=dev["O"], device_id_type=MESH,
        )

    if COMM:
        for d in range(1, 16):
            q = lax.rem(q_me + d, 16)
            pltpu.make_async_remote_copy(
                src_ref=ar_src.at[q], dst_ref=ar_one.at[q_me],
                send_sem=ar_send.at[0], recv_sem=ar_recv.at[0],
                device_id=group_one(q), device_id_type=MESH,
            ).start()

    def extra(j):
        return pltpu.make_async_remote_copy(
            src_ref=ar_src.at[16 + j], dst_ref=ex_one.at[q_me],
            send_sem=ar_send.at[3 + j], recv_sem=ar_recv.at[3],
            device_id=group_one(j), device_id_type=MESH,
        )

    def extra_final(j):
        return pltpu.make_async_remote_copy(
            src_ref=ex_three.at[j], dst_ref=ex_three.at[j],
            send_sem=ar_send.at[6], recv_sem=ar_recv.at[5 + j],
            device_id=dev["W"], device_id_type=MESH,
        )

    for j in range(2):
        @pl.when(q_me == j)
        def _():
            ex_one[pl.ds(j, 1)] = ar_src[pl.ds(16 + j, 1)]

        if COMM:
            pl.when(q_me != j)(extra(j).start)

    def middle():
        if COMM:
            batch(ar_one, 15, 0).wait_recv()
        ar_mid[...] = jnp.sum(ar_one[...].astype(F32), axis=0).astype(BF16)
        ar_two[pl.ds(p_me, 1)] = ar_mid[...][None]
        if COMM:
            for d in range(1, 8):
                pltpu.make_async_remote_copy(
                    src_ref=ar_mid, dst_ref=ar_two.at[p_me],
                    send_sem=ar_send.at[1], recv_sem=ar_recv.at[1],
                    device_id=group_two(lax.rem(p_me + d, 8)), device_id_type=MESH,
                ).start()

            @pl.when(q_me < 2)
            def _():
                batch(ex_one, 15, 3).wait_recv()
                ex_mid[...] = jnp.sum(ex_one[...].astype(F32), axis=0).astype(BF16)
                ex_two[pl.ds(p_me, 1)] = ex_mid[...][None]
                for d in range(1, 8):
                    pltpu.make_async_remote_copy(
                        src_ref=ex_mid, dst_ref=ex_two.at[p_me],
                        send_sem=ar_send.at[5], recv_sem=ar_recv.at[4],
                        device_id=group_two(lax.rem(p_me + d, 8)), device_id_type=MESH,
                    ).start()

    def collect():
        if COMM:
            batch(ar_two, 7, 1).wait_recv()
        final = jnp.sum(ar_two[...].astype(F32), axis=0).astype(BF16)
        ar_three[pl.ds(q_me, 1)] = final[None]
        if COMM:
            for d in range(1, 16):
                pltpu.make_async_remote_copy(
                    src_ref=ar_three.at[q_me], dst_ref=ar_three.at[q_me],
                    send_sem=ar_send.at[2], recv_sem=ar_recv.at[2],
                    device_id=group_one(lax.rem(q_me + d, 16)), device_id_type=MESH,
                ).start()

            for j in range(2):
                @pl.when(q_me == j)
                def _():
                    batch(ex_two, 7, 4).wait_recv()
                    ex_three[j] = jnp.sum(ex_two[...].astype(F32), axis=0).astype(BF16)
                    for d in range(1, 16):
                        pltpu.make_async_remote_copy(
                            src_ref=ex_three.at[j], dst_ref=ex_three.at[j],
                            send_sem=ar_send.at[6], recv_sem=ar_recv.at[5 + j],
                            device_id=group_one((j + d) % 16), device_id_type=MESH,
                        ).start()

    def finish():
        if COMM:
            batch(ar_three, 15, 2).wait_recv()
            for j in range(2):
                pl.when(q_me != j)(extra_final(j).wait_recv)
        for q in range(16):
            chunk = ar_three[q].astype(F32)
            grad_wvalue[8 * q : 8 * q + 8, :] = chunk[0:8]
            grad_wout[8 * q : 8 * q + 8, :] = chunk[8:16]
        grad_gain[...] = ex_three[0].astype(F32)
        grad_wradial[...] = ex_three[1].astype(F32)[:K]

    for c in range(2):
        for k in range(K):
            lhs[c, k, :, :N] = (grad_agg[c] * wk[k : k + 1]).astype(BF16)
        pacc[c] = jnp.zeros((3, N, N), F32)

    def pulls(c, role, part=ALL):
        low, high = part[c]
        wide = high - low
        rows = 64 // wide if wide < 3 else ROWS
        span = slice((c + low) * N, (c + high) * N)
        lanes = slice(low * N, high * N)
        both = jnp.concatenate([hc[role, span, :], hg[role, span, :]], axis=1)
        sbuf[:, :, : wide * N] = dot(lhs[c].reshape(K * N, 2 * N), both, ((1,), (1,))).reshape(K, N, wide * N)
        near_rows = [row[:, lanes] for row in near(c, role)]

        @pl.loop(0, N // rows)
        def _(i):
            some = pl.ds(pl.multiple_of(i * rows, rows), rows)
            ratio = geo[c, role, 0, some, lanes]
            total = sbuf[K - 1, some, : wide * N]
            slope = total
            for k in range(K - 2, -1, -1):
                total = total * ratio + sbuf[k, some, : wide * N]
                if k > 0:
                    slope = slope * ratio + total
            slope = slope * ratio
            pull = geo[c, role, 1, some, lanes] * total - geo[c, role, 2, some, lanes] * slope
            for n in range(3):
                mine = own[c, n, some, :]
                moved = pacc[c, n, some, :]
                for w in range(wide):
                    block = slice(w * N, (w + 1) * N)
                    moved = moved + pull[:, block] * (near_rows[n][:, block] - mine)
                pacc[c, n, some, :] = moved

    for c in range(2):
        out_feat[0, c] = (hf[0, own_rows(c), :].astype(F32) + pre[c] * sigs[c]).astype(BF16)
    for c in range(2):
        gather(c, 0, hg, True, EARLY)
    for c in range(2):
        pulls(c, 0, EARLY)
    if COMM:
        for who, copy in sent[:early_sent]:
            where_sent(who, copy.wait_send)
    middle()
    arrive(GRAD, (0, 0), (0, 3))
    for c in range(2):
        gather(c, 0, hg, False, LATE)
    for c in range(2):
        pulls(c, 0, LATE)
    for col in (1, 2):
        arrive(GRAD, (1, col))
        send(GRAD, RELAY[col])
    for c in range(2):
        gather(c, 1, hg, False, EARLY)
    for c in range(2):
        pulls(c, 1, EARLY)
    collect()
    arrive(GRAD, (1, 0), (1, 3))
    for c in range(2):
        gather(c, 1, hg, False, LATE)
    for c in range(2):
        pulls(c, 1, LATE)
    arrive(GRAD, (2, 0), (2, 1), (2, 2), (2, 3))
    for c in range(2):
        gather(c, 2, hg, False)
    for c in range(2):
        pulls(c, 2)

    for c in range(2):
        total = usum[c, 0] * wk[0:1]
        for k in range(1, K):
            total = total + usum[c, k] * wk[k : k + 1]
        back = (total * gain[0, own_rows(c), :]).astype(BF16)
        change = dot(back, w_value[...], ((1,), (1,)))
        grad_feat[0, c] = (cot[0, c].astype(F32) + change).astype(BF16)
        for n in range(3):
            scale = 2.0 * (HZ if n == 2 else 1.0)
            grad_pos[0, n, c : c + 1, :] = jnp.sum(pacc[c, n].T, axis=0, keepdims=True) * scale
    if COMM:
        for who, copy in sent[early_sent:]:
            where_sent(who, copy.wait_send)
        batch(ar_one, 15, 0).wait_send()
        batch(ar_two, 7, 1).wait_send()
    finish()
    if COMM:
        batch(ar_three, 15, 2).wait_send()
        for j in range(2):
            pl.when(q_me != j)(extra(j).wait_send)

        @pl.when(q_me < 2)
        def _():
            pltpu.make_async_remote_copy(
                src_ref=ex_two.at[pl.ds(0, 7)], dst_ref=ex_two.at[pl.ds(0, 7)],
                send_sem=ar_send.at[5], recv_sem=ar_recv.at[4], device_id=dev["W"], device_id_type=MESH,
            ).wait_send()
            pltpu.make_async_remote_copy(
                src_ref=ex_one.at[pl.ds(0, 15)], dst_ref=ex_one.at[pl.ds(0, 15)],
                send_sem=ar_send.at[6], recv_sem=ar_recv.at[3], device_id=dev["W"], device_id_type=MESH,
            ).wait_send()


def store(*refs):
    count = len(refs) // 2
    sems = refs[-1]
    copies = [pltpu.make_async_copy(refs[n], refs[count + n], sems.at[n]) for n in range(count)]
    for copy in copies:
        copy.start()
    for copy in copies:
        copy.wait()


def on_device(features, positions, bead_types, cell_counts, w_value, w_radial, type_gain, w_out, cotangent):
    vmem = pl.BlockSpec(memory_space=pltpu.VMEM)
    anywhere = pl.BlockSpec(memory_space=pl.ANY)
    shape = jax.ShapeDtypeStruct
    shapes = (
        shape((1, 2, N, N), BF16),
        shape((1, 2, N, N), BF16),
        shape((1, 3, 2, N), F32),
        shape((N, N), F32),
        shape((K, N), F32),
        shape((16, N), F32),
        shape((N, N), F32),
    )
    results = pl.pallas_call(
        kernel,
        out_shape=shapes,
        in_specs=[pl.BlockSpec(memory_space=pltpu.HBM)] * 9,
        out_specs=(vmem,) * 7,
        scratch_shapes=[
            pltpu.VMEM((3, 8, 4 * N), F32),
            pltpu.VMEM((3, 4 * N, N), BF16),
            pltpu.VMEM((3, 4 * N, N), BF16),
            pltpu.VMEM((3, 4 * N, N), BF16),
            pltpu.VMEM((2, 3, N, N), F32),
            pltpu.VMEM((2, 3, K, N, 3 * N), BF16),
            pltpu.VMEM((2, 3, 3, N, 3 * N), F32),
            pltpu.VMEM((2, K, N, N), F32),
            pltpu.VMEM((K, N, 3 * N), F32),
            pltpu.VMEM((2, K, N, 2 * N), BF16),
            pltpu.VMEM((2, 3, N, N), F32),
            pltpu.VMEM((3, 4 * N, N), F32),
            pltpu.VMEM((3, 4 * N, N), F32),
            pltpu.VMEM((3, 16, 4 * N), F32),
            pltpu.VMEM((K, N, N), F32),
            pltpu.VMEM((2, N, K * N), BF16),
            pltpu.VMEM((3, N, 4 * N), F32),
            pltpu.VMEM((1, 3, 2, N), F32),
            pltpu.VMEM((1, 2, N), jnp.int32),
            pltpu.VMEM((1, 2), jnp.int32),
            pltpu.VMEM((N, N), BF16),
            pltpu.VMEM((K, N), F32),
            pltpu.VMEM((16, N), F32),
            pltpu.VMEM((N, N), BF16),
            pltpu.VMEM((1, 2, N, N), BF16),
            pltpu.VMEM((18, 16, N), BF16),
            pltpu.VMEM((16, 16, N), BF16),
            pltpu.VMEM((16, N), BF16),
            pltpu.VMEM((8, 16, N), BF16),
            pltpu.VMEM((16, 16, N), BF16),
            pltpu.VMEM((16, 16, N), BF16),
            pltpu.VMEM((16, N), BF16),
            pltpu.VMEM((8, 16, N), BF16),
            pltpu.VMEM((2, 16, N), BF16),
            pltpu.SemaphoreType.DMA((10,)),
            pltpu.SemaphoreType.DMA((42,)),
            pltpu.SemaphoreType.DMA((3, 12)),
            pltpu.SemaphoreType.DMA((7,)),
            pltpu.SemaphoreType.DMA((7,)),
        ],
        compiler_params=pltpu.CompilerParams(
            collective_id=0, has_side_effects=True, vmem_limit_bytes=40 * 1024 * 1024
        ),
        cost_estimate=pl.CostEstimate(flops=4_000_000_000, bytes_accessed=1_000_000, transcendentals=4_000_000),
    )(*(pltpu.with_memory_space_constraint(array, pltpu.HBM) for array in (
        features, positions.transpose(0, 2, 1, 3), bead_types, cell_counts,
        w_value, w_radial, type_gain, w_out, cotangent,
    )))
    out = pl.pallas_call(
        store,
        out_shape=shapes,
        in_specs=[anywhere] * 7,
        out_specs=(pl.BlockSpec(memory_space=pltpu.HBM),) * 7,
        scratch_shapes=[pltpu.SemaphoreType.DMA((7,))],
        compiler_params=pltpu.CompilerParams(vmem_limit_bytes=2 * 1024 * 1024),
    )(*results)
    return (out[0], out[1], out[2].transpose(0, 2, 1, 3)) + tuple(out[3:])


def solution(mesh):
    cells = P(("frame", "gx"), "gy", None, None)
    return jax.shard_map(
        on_device,
        mesh=mesh,
        in_specs=(cells, cells, P(("frame", "gx"), "gy", None), P(("frame", "gx"), "gy"), P(), P(), P(), P(), cells),
        out_specs=(cells, cells, cells) + (P("frame", None),) * 4,
        check_vma=False,
    )
```
